128 devices in a mesh: lat: 8 (over z_hi, y), lon: 16 (over z_lo, x, core).
Axes of the slice: x: 4, y: 4, z: 4 (z_hi: 2, z_lo: 2; z = z_hi * 2 + z_lo), core: 2. Of those that a mesh axis runs over, the one named last changes fastest.
Arguments:
- tokens: bfloat16 [512, 768, 512], P('lat', 'lon'), may hold values from -8 to 8
- gain_attn1: float32 [512], replicated, may hold values from 0.1 to 1.9
- w_qkv1: bfloat16 [512, 1536], replicated, may hold values from -8 to 8
- w_out1: bfloat16 [512, 512], replicated, may hold values from -0.25 to 0.25
- gain_mlp1: float32 [512], replicated, may hold values from 0.1 to 1.9
- w_up: bfloat16 [512, 2048], replicated, may hold values from -0.25 to 0.25
- w_down: bfloat16 [2048, 512], replicated, may hold values from -0.125 to 0.125
- gain_merge: float32 [2048], replicated, may hold values from 0.1 to 1.9
- w_merge: bfloat16 [2048, 1024], replicated, may hold values from -0.125 to 0.125
- gain_attn2: float32 [1024], replicated, may hold values from 0.1 to 1.9
- w_qkv2: bfloat16 [1024, 3072], replicated, may hold values from -8 to 8
- w_out2: bfloat16 [1024, 1024], replicated, may hold values from -0.1875 to 0.1875
Outputs:
- coarse_out: bfloat16 [256, 384, 1024], P('lat', 'lon')
The draws below stay inside these ranges and needn't reach their ends.
All inputs are finite; a program needn't handle non-finite values.
Results may differ from the reference program's by a relative error of at most 0.017.
Values may be sent and summed in bfloat16 or wider, within the bound.
No kernel may reach another device: no remote copies, remote signals or barrier semaphores. Data moves between devices by JAX's collectives and lax.ppermute only.
A program may use at most 128 MiB of HBM per device.

```python
import jax
import jax.numpy as jnp
from jax import lax

C1 = 512
C2 = 1024
MLP1 = 2048
HEAD_DIM = 64
WIN = 8
HALF = 4
NLAT = 512
NLON = 768


def draw_tokens(key, part):
    key = jax.random.fold_in(key, 11)
    shape = (NLAT, NLON, C1)
    return jax.random.truncated_normal(key, -6.0, 6.0, shape, jnp.float32).astype(jnp.bfloat16)


def projection_draw(key, channels, strengths):
    query_key, keys_key, value_key = jax.random.split(key, 3)
    factor = channels ** (-0.5)
    queries = jax.random.truncated_normal(query_key, -4.0, 4.0, (channels, channels), jnp.float32) * factor
    own_keys = jax.random.truncated_normal(keys_key, -4.0, 4.0, (channels, channels), jnp.float32) * factor
    values = jax.random.truncated_normal(value_key, -4.0, 4.0, (channels, channels), jnp.float32) * factor
    column_strength = jnp.repeat(strengths, HEAD_DIM)
    keys_out = queries * column_strength[None, :] + own_keys
    return jnp.clip(jnp.concatenate([queries, keys_out, values], axis=1), -8.0, 8.0)


def draw_w_qkv1(key, part):
    key = jax.random.fold_in(key, 21)
    matrix_key = jax.random.fold_in(key, 1)
    strengths = jnp.zeros((C1 // HEAD_DIM,), jnp.float32)
    return projection_draw(matrix_key, C1, strengths).astype(jnp.bfloat16)


def draw_w_qkv2(key, part):
    key = jax.random.fold_in(key, 31)
    matrix_key = jax.random.fold_in(key, 1)
    strengths = jnp.zeros((C2 // HEAD_DIM,), jnp.float32)
    return projection_draw(matrix_key, C2, strengths).astype(jnp.bfloat16)


def gaussian(key, extent, scale, most, held_as=jnp.bfloat16):
    entries = scale * jax.random.normal(key, extent, jnp.float32)
    return jnp.clip(entries, min=-most, max=most).astype(held_as)


def setup_inputs(seed: int = 0) -> dict:
    streams_of = jax.random.split(jax.random.key(seed), 13)
    tokens = draw_tokens(jax.random.fold_in(streams_of[12], 71), 0)
    gain_attn1 = jnp.clip(1.0 + 0.18 * jax.random.normal(streams_of[1], (C1,), jnp.float32), 0.1, 1.9)
    w_qkv1 = draw_w_qkv1(jax.random.fold_in(streams_of[12], 71), 0)
    w_out1 = gaussian(streams_of[3], (C1, C1), C1 ** -0.5, 0.25)
    gain_mlp1 = jnp.clip(1.0 + 0.18 * jax.random.normal(streams_of[4], (C1,), jnp.float32), 0.1, 1.9)
    w_up = gaussian(streams_of[5], (C1, MLP1), C1 ** -0.5, 0.25)
    w_down = gaussian(streams_of[6], (MLP1, C1), MLP1 ** -0.5, 0.125)
    gain_merge = jnp.clip(1.0 + 0.18 * jax.random.normal(streams_of[7], (4 * C1,), jnp.float32), 0.1, 1.9)
    w_merge = gaussian(streams_of[8], (4 * C1, C2), (4 * C1) ** -0.5, 0.125)
    gain_attn2 = jnp.clip(1.0 + 0.18 * jax.random.normal(streams_of[9], (C2,), jnp.float32), 0.1, 1.9)
    w_qkv2 = draw_w_qkv2(jax.random.fold_in(streams_of[12], 71), 0)
    w_out2 = gaussian(streams_of[11], (C2, C2), C2 ** -0.5, 0.1875)
    return dict(tokens=tokens, gain_attn1=gain_attn1, w_qkv1=w_qkv1, w_out1=w_out1, gain_mlp1=gain_mlp1, w_up=w_up, w_down=w_down, gain_merge=gain_merge, w_merge=w_merge, gain_attn2=gain_attn2, w_qkv2=w_qkv2, w_out2=w_out2)


def layer_norm(values, scales):
    average = lax.optimization_barrier(jnp.mean(values, axis=-1, keepdims=True))
    centred = values - average
    spread = lax.optimization_barrier(jnp.mean(centred * centred, axis=-1, keepdims=True))
    return centred * lax.rsqrt(spread + 1e-05) * scales

def attend(queries, keys_in, values_in, key_ok):
    scores = jnp.einsum('wphd,wqhd->whpq', queries.astype(jnp.float32), keys_in.astype(jnp.float32)) * HEAD_DIM ** (-0.5)
    scores = jnp.where(key_ok[:, None, None, :], scores, -1e+30)
    largest = lax.optimization_barrier(jnp.max(scores, axis=-1, keepdims=True))
    weights = jnp.exp(scores - largest)
    shares = (weights / lax.optimization_barrier(jnp.sum(weights, axis=-1, keepdims=True))).astype(jnp.bfloat16)
    result = jnp.einsum('whpq,wqhd->wphd', shares.astype(jnp.float32), values_in.astype(jnp.float32))
    return result.astype(jnp.bfloat16).reshape(result.shape[0], result.shape[1], -1)

def attention_block(inputs, scales, w_qkv, w_out):
    height, breadth, channels = inputs.shape
    head_count = channels // HEAD_DIM
    padded = jnp.pad(inputs, ((HALF, HALF), (0, 0), (0, 0)))
    padded = jnp.roll(padded, HALF, axis=1)
    row_valid = jnp.pad(jnp.ones((height,), jnp.float32), (HALF, HALF))
    row_count = (height + 2 * HALF) // WIN
    col_count = breadth // WIN
    window_rows = padded.reshape(row_count, WIN, breadth, channels)
    rows_valid = row_valid.reshape(row_count, WIN)

    def one_band(operands):
        band, valid_rows = operands
        normed = layer_norm(band.astype(jnp.float32), scales).astype(jnp.bfloat16)
        projected = jnp.dot(normed.reshape(WIN * breadth, channels), w_qkv, preferred_element_type=jnp.float32).astype(jnp.bfloat16)
        projected = projected.reshape(WIN, col_count, WIN, 3 * channels).transpose(1, 0, 2, 3)
        projected = projected.reshape(col_count, WIN * WIN, 3, head_count, HEAD_DIM)
        key_ok = jnp.broadcast_to(valid_rows[:, None], (WIN, WIN)).reshape(WIN * WIN) > 0.5
        key_ok = jnp.broadcast_to(key_ok[None, :], (col_count, WIN * WIN))
        result = attend(projected[:, :, 0], projected[:, :, 1], projected[:, :, 2], key_ok)
        result = result.reshape(col_count, WIN, WIN, channels).transpose(1, 0, 2, 3).reshape(WIN * breadth, channels)
        update = jnp.dot(result, w_out, preferred_element_type=jnp.float32)
        total = band.astype(jnp.float32).reshape(WIN * breadth, channels) + update
        return total.astype(jnp.bfloat16).reshape(WIN, breadth, channels)
    outputs = lax.map(one_band, (window_rows, rows_valid))
    outputs = outputs.reshape(row_count * WIN, breadth, channels)
    return jnp.roll(outputs, -HALF, axis=1)[HALF:HALF + height]

def reference(tokens, gain_attn1, w_qkv1, w_out1, gain_mlp1, w_up, w_down, gain_merge, w_merge, gain_attn2, w_qkv2, w_out2):
    hidden_state = attention_block(tokens, gain_attn1, w_qkv1, w_out1)

    def mlp_line(line_in):
        normed = layer_norm(line_in.astype(jnp.float32), gain_mlp1).astype(jnp.bfloat16)
        inner = jax.nn.gelu(jnp.dot(normed, w_up, preferred_element_type=jnp.float32)).astype(jnp.bfloat16)
        total = line_in.astype(jnp.float32) + jnp.dot(inner, w_down, preferred_element_type=jnp.float32)
        return total.astype(jnp.bfloat16)
    refined = lax.map(mlp_line, hidden_state)
    quads = jnp.concatenate([refined[0::2, 0::2], refined[1::2, 0::2], refined[0::2, 1::2], refined[1::2, 1::2]], axis=-1)

    def merge_line(line_in):
        normed = layer_norm(line_in.astype(jnp.float32), gain_merge).astype(jnp.bfloat16)
        return jnp.dot(normed, w_merge, preferred_element_type=jnp.float32).astype(jnp.bfloat16)
    coarse = lax.map(merge_line, quads)
    return attention_block(coarse, gain_attn2, w_qkv2, w_out2)
```

```python
import functools

import jax
import jax.numpy as jnp
import numpy as np
from jax import lax
from jax.experimental import pallas as pl
from jax.experimental.pallas import tpu as pltpu
from jax.sharding import PartitionSpec as P

HEAD_DIM = 64
WIN = 8
HALF = 4
TOK = WIN * WIN
QUAD = 4 * HEAD_DIM
ROWS, COLS, C1 = 64, 48, 512
MLP1 = 2048
C2 = 1024
CROWS, CCOLS = ROWS // 2, COLS // 2
BANDS, BWIN = ROWS // WIN, COLS // WIN
BTOK = WIN * COLS
CTOK = CROWS * CCOLS
CBANDS, CBWIN = CROWS // WIN, CCOLS // WIN
SCALE = HEAD_DIM**-0.5 * 1.4426950408889634
F32 = jnp.float32
BF16 = jnp.bfloat16


def band_source():
    out = np.zeros((BTOK, 1), np.int32)
    for o in range(BTOK):
        w, t = divmod(o, TOK)
        r = 2 * ((t >> 2) & 3) + ((t >> 4) & 1)
        c = WIN * w + 2 * (t & 3) + (t >> 5) + HALF
        out[o] = r * COLS + c if c < COLS else BTOK + r * HALF + c - COLS
    return out


def coarse_place(r, c):
    return ((r // 4) * BWIN + c // 4) * 16 + (r % 4) * 4 + c % 4


def coarse_send_source():
    out = np.full((128, 1), -1, np.int32)
    for i in range(2 * CCOLS):
        out[i] = coarse_place(i // CCOLS, i % CCOLS)
    for i in range(2 * CROWS):
        out[48 + i] = coarse_place(i // 2, i % 2)
    for i in range(4):
        out[112 + i] = coarse_place(i // 2, i % 2)
    return out


def coarse_source():
    out = np.zeros((CTOK, 1), np.int32)
    for o in range(CTOK):
        w, t = divmod(o, TOK)
        r = WIN * (w // CBWIN) + t // WIN + 2
        c = WIN * (w % CBWIN) + t % WIN + 2
        if r < CROWS and c < CCOLS:
            out[o] = coarse_place(r, c)
        elif c < CCOLS:
            out[o] = CTOK + (r - CROWS) * CCOLS + c
        elif r < CROWS:
            out[o] = CTOK + 48 + r * 2 + c - CCOLS
        else:
            out[o] = CTOK + 112 + (r - CROWS) * 2 + c - CCOLS
    return out


def window_place(r, c):
    return ((r // WIN) * CBWIN + c // WIN) * TOK + (r % WIN) * WIN + c % WIN


def result_source():
    out = np.full((976, 1), -1, np.int32)
    for r in range(HALF, CROWS):
        for c in range(HALF, CCOLS):
            out[r * CCOLS + c] = window_place(r - HALF, c - HALF)
    at = CTOK
    for r in range(CROWS - HALF, CROWS):
        for c in range(CCOLS - HALF):
            out[at] = window_place(r, c)
            at += 1
    for r in range(CROWS - HALF):
        for c in range(CCOLS - HALF, CCOLS):
            out[at] = window_place(r, c)
            at += 1
    for r in range(CROWS - HALF, CROWS):
        for c in range(CCOLS - HALF, CCOLS):
            out[at] = window_place(r, c)
            at += 1
    return out


def rim_source():
    out = np.full((CTOK, 1), -1, np.int32)
    for r in range(CROWS):
        for c in range(CCOLS):
            if r < HALF and c >= HALF:
                out[r * CCOLS + c] = r * (CCOLS - HALF) + c - HALF
            elif r >= HALF and c < HALF:
                out[r * CCOLS + c] = 80 + (r - HALF) * HALF + c
            elif r < HALF:
                out[r * CCOLS + c] = 192 + r * HALF + c
    return out


def picks(source, width):
    lanes = lax.broadcasted_iota(jnp.int32, (source.shape[0], width), 1)
    return (lanes == source).astype(F32).astype(BF16)


def layer_norm(values, scales):
    average = jnp.mean(values, axis=-1, keepdims=True)
    centred = values - average
    spread = jnp.mean(centred * centred, axis=-1, keepdims=True)
    return centred * lax.rsqrt(spread + 1e-05) * scales


def gelu(x):
    return 0.5 * x * (1.0 + jnp.tanh(x * (0.7978845608028654 + 0.035677408136300125 * (x * x))))


def dot(a, b):
    return jnp.dot(a, b, preferred_element_type=F32)


def head_blocks():
    rows = lax.broadcasted_iota(jnp.int32, (QUAD, QUAD), 0) // HEAD_DIM
    lanes = lax.broadcasted_iota(jnp.int32, (QUAD, QUAD), 1) // HEAD_DIM
    return (rows == lanes).astype(F32).astype(BF16)


def attend(queries, keys_in, values_in, blocks, bias):
    spread = jnp.concatenate([queries] * 4, axis=0) * blocks
    scores = lax.dot_general(keys_in, spread, (((1,), (1,)), ((), ())), preferred_element_type=F32)
    scores = scores * SCALE + bias
    weights = jnp.exp2(scores - jnp.max(scores, axis=0, keepdims=True))
    shares = (weights * (1.0 / jnp.sum(weights, axis=0, keepdims=True))).astype(BF16)
    mixed = lax.dot_general(shares, values_in, (((0,), (0,)), ((), ())), preferred_element_type=F32)
    low = lax.broadcasted_iota(jnp.int32, (TOK, 128), 1) < HEAD_DIM
    left = jnp.where(low, mixed[0:64, 0:128], mixed[64:128, 0:128])
    right = jnp.where(low, mixed[128:192, 128:256], mixed[192:256, 128:256])
    return jnp.concatenate([left, right], axis=1).astype(BF16)


def section_one(
    x_hbm, hr_hbm, he_hbm, hx_hbm, wqkv_hbm, wout_hbm, wup_hbm, wdown_hbm, wmerge_hbm,
    flag, gain_attn, gain_mlp, gain_merge, source, send_source,
    coarse, send_rows, send_cols, send_corner,
    xs, hcs, wqkv, wout, wup, wdown, wmerge, perm, blocks, qkv, attended, merged, sems,
):
    band = pl.program_id(0)
    pairs = (
        (x_hbm, xs.at[0:ROWS]), (hr_hbm, xs.at[ROWS : ROWS + HALF]), (he_hbm, hcs.at[0:240]), (hx_hbm, hcs.at[240:256]),
        (wqkv_hbm, wqkv), (wout_hbm, wout), (wup_hbm, wup), (wdown_hbm, wdown), (wmerge_hbm, wmerge),
    )
    copies = [pltpu.make_async_copy(a, b, sems.at[i]) for i, (a, b) in enumerate(pairs)]

    @pl.when(band == 0)
    def _():
        for c in copies:
            c.start()
        perm[...] = picks(source[...], BTOK + 32)
        blocks[...] = head_blocks()
        for c in copies[:8]:
            c.wait()

    top = band * WIN + HALF
    raw = xs[pl.ds(top, WIN)].reshape(BTOK, C1)
    rim = hcs[pl.ds(pl.multiple_of(band * 32, 32), 32)]
    tokens = dot(perm[...], jnp.concatenate([raw, rim], axis=0))
    normed = layer_norm(tokens, gain_attn[...]).astype(BF16)
    for n in range(0, 3 * C1, 512):
        qkv[:, n : n + 512] = dot(normed, wqkv[:, n : n + 512]).astype(BF16)
    half_of = lambda axis: (lax.broadcasted_iota(jnp.int32, (TOK, QUAD), axis) >> 3) & 1
    cut = jnp.where((flag[0] == 1) & (band == BANDS - 1), -1e30, 0.0)
    bias = (half_of(0) != half_of(1)).astype(F32) * cut
    for w in range(BWIN):
        here = slice(w * TOK, w * TOK + TOK)
        for g in range(C1 // QUAD):
            attended[here, g * QUAD : g * QUAD + QUAD] = attend(
                qkv[here, g * QUAD : g * QUAD + QUAD],
                qkv[here, C1 + g * QUAD : C1 + g * QUAD + QUAD],
                qkv[here, 2 * C1 + g * QUAD : 2 * C1 + g * QUAD + QUAD],
                blocks[...], bias,
            )
    hidden = (tokens + dot(attended[...], wout[...])).astype(BF16).astype(F32)
    normed = layer_norm(hidden, gain_mlp[...]).astype(BF16)
    total = hidden
    for n in range(0, MLP1, 512):
        inner = gelu(dot(normed, wup[:, n : n + 512])).astype(BF16)
        total = total + dot(inner, wdown[n : n + 512, :])
    refined = total.astype(BF16).astype(F32).reshape(BWIN, 4, 16, C1)
    quads = jnp.concatenate([refined[:, i] for i in range(4)], axis=-1).reshape(BTOK // 4, 4 * C1)
    merged[pl.ds(pl.multiple_of(band * (BTOK // 4), BTOK // 4), BTOK // 4), :] = layer_norm(quads, gain_merge[...]).astype(BF16)

    @pl.when(band == BANDS - 1)
    def _():
        copies[8].wait()
        for n in range(0, C2, 256):
            coarse[:, n : n + 256] = dot(merged[...], wmerge[:, n : n + 256]).astype(BF16)
        sent = dot(picks(send_source[...], CTOK), coarse[...]).astype(BF16)
        send_rows[...] = sent[0:48]
        send_cols[...] = sent[48:112]
        send_corner[...] = sent[112:128]


def section_two(
    own_hbm, hr_hbm, hc_hbm, hx_hbm, wqkv_hbm, wout_hbm, flag, gain, source, out_source,
    main, send_rows, send_cols, send_corner,
    ext, wqkv, wout, blocks, held, normed, qkv, attended, result, sems,
):
    pairs = (
        (own_hbm, ext.at[0:CTOK]), (hr_hbm, ext.at[768:816]), (hc_hbm, ext.at[816:880]), (hx_hbm, ext.at[880:896]),
        (wqkv_hbm, wqkv), (wout_hbm, wout),
    )
    copies = [pltpu.make_async_copy(a, b, sems.at[i]) for i, (a, b) in enumerate(pairs)]
    for c in copies:
        c.start()
    blocks[...] = head_blocks()
    for c in copies[:4]:
        c.wait()
    for i in range(CBANDS):
        here = slice(i * 192, i * 192 + 192)
        tokens = dot(picks(source[here], 896), ext[...])
        held[here] = tokens.astype(BF16)
        normed[here] = layer_norm(tokens, gain[...]).astype(BF16)
    copies[4].wait()
    for n in range(0, 3 * C2, 512):
        qkv[:, n : n + 512] = dot(normed[...], wqkv[:, n : n + 512]).astype(BF16)

    def one_band(i, carry):
        half_of = lambda axis: (lax.broadcasted_iota(jnp.int32, (TOK, QUAD), axis) >> 5) & 1
        cut = jnp.where((flag[0] == 1) & (i == CBANDS - 1), -1e30, 0.0)
        bias = (half_of(0) != half_of(1)).astype(F32) * cut
        for w in range(CBWIN):
            here = pl.ds(pl.multiple_of(i * 192 + w * TOK, TOK), TOK)
            for g in range(C2 // QUAD):
                attended[here, g * QUAD : g * QUAD + QUAD] = attend(
                    qkv[here, g * QUAD : g * QUAD + QUAD],
                    qkv[here, C2 + g * QUAD : C2 + g * QUAD + QUAD],
                    qkv[here, 2 * C2 + g * QUAD : 2 * C2 + g * QUAD + QUAD],
                    blocks[...], bias,
                )
        return carry

    lax.fori_loop(0, CBANDS, one_band, 0)
    copies[5].wait()
    for n in range(0, C2, 256):
        here = slice(n, n + 256)
        result[:, here] = (held[:, here].astype(F32) + dot(attended[...], wout[:, here])).astype(BF16)
    for i in range(CBANDS):
        here = slice(i * 192, i * 192 + 192)
        main[here] = dot(picks(out_source[here], CTOK), result[...]).astype(BF16)
    sent = dot(picks(out_source[CTOK:], CTOK), result[...]).astype(BF16)
    send_rows[...] = sent[0:80]
    send_cols[...] = sent[80:192]
    send_corner[...] = sent[192:208]


def join(main, rows, cols, corner, source, out):
    rim = jnp.concatenate([rows[...], cols[...], corner[...]], axis=0)
    out[...] = (main[...].astype(F32) + dot(picks(source[...], 208), rim)).astype(BF16)


ANY = pl.BlockSpec(memory_space=pl.ANY)
VM = pl.BlockSpec(memory_space=pltpu.VMEM)
SM = pl.BlockSpec(memory_space=pltpu.SMEM)


def whole(shape):
    return pl.BlockSpec(shape, lambda b: (0,) * len(shape))


def shift(values, axes, back):
    if isinstance(axes, str):
        count = lax.axis_size(axes)
        pairs = [(i, (i + 1) % count) for i in range(count)]
    else:
        lat, lon = (lax.axis_size(a) for a in axes)
        pairs = [(i * lon + j, ((i + 1) % lat) * lon + (j + 1) % lon) for i in range(lat) for j in range(lon)]
    if back:
        pairs = [(b, a) for a, b in pairs]
    return lax.ppermute(values, axes, pairs)


def on_device(
    tokens, gain_attn1, w_qkv1, w_out1, gain_mlp1, w_up, w_down, gain_merge, w_merge, gain_attn2, w_qkv2, w_out2,
):
    flag = (lax.axis_index("lat") == lax.axis_size("lat") - 1).astype(jnp.int32).reshape(1)
    rim_r = shift(tokens[0:HALF], "lat", True)
    rim_c = shift(tokens[HALF:, 0:HALF].reshape(240, C1), "lon", True)
    rim_x = shift(tokens[0:HALF, 0:HALF].reshape(16, C1), ("lat", "lon"), True)
    sds = jax.ShapeDtypeStruct
    coarse, s_r, s_c, s_x = pl.pallas_call(
        section_one,
        grid=(BANDS,),
        out_shape=[sds((CTOK, C2), BF16), sds((48, C2), BF16), sds((64, C2), BF16), sds((16, C2), BF16)],
        in_specs=[ANY] * 9 + [SM, whole((1, C1)), whole((1, C1)), whole((1, 4 * C1)), whole((BTOK, 1)), whole((128, 1))],
        out_specs=[whole((CTOK, C2)), whole((48, C2)), whole((64, C2)), whole((16, C2))],
        scratch_shapes=[
            pltpu.VMEM((ROWS + HALF, COLS, C1), BF16),
            pltpu.VMEM((256, C1), BF16),
            pltpu.VMEM((C1, 3 * C1), BF16),
            pltpu.VMEM((C1, C1), BF16),
            pltpu.VMEM((C1, MLP1), BF16),
            pltpu.VMEM((MLP1, C1), BF16),
            pltpu.VMEM((4 * C1, C2), BF16),
            pltpu.VMEM((BTOK, BTOK + 32), BF16),
            pltpu.VMEM((QUAD, QUAD), BF16),
            pltpu.VMEM((BTOK, 3 * C1), BF16),
            pltpu.VMEM((BTOK, C1), BF16),
            pltpu.VMEM((CTOK, 4 * C1), BF16),
            pltpu.SemaphoreType.DMA((9,)),
        ],
        compiler_params=pltpu.CompilerParams(vmem_limit_bytes=56 << 20),
        name="section_one",
    )(
        tokens, rim_r, rim_c, rim_x, w_qkv1, w_out1, w_up, w_down, w_merge,
        flag, gain_attn1.reshape(1, -1), gain_mlp1.reshape(1, -1), gain_merge.reshape(1, -1),
        jnp.asarray(band_source()), jnp.asarray(coarse_send_source()),
    )
    r_r = shift(s_r, "lat", True)
    r_c = shift(s_c, "lon", True)
    r_x = shift(s_x, ("lat", "lon"), True)
    main, s_r, s_c, s_x = pl.pallas_call(
        section_two,
        out_shape=[sds((CTOK, C2), BF16), sds((80, C2), BF16), sds((112, C2), BF16), sds((16, C2), BF16)],
        in_specs=[ANY] * 6 + [SM, VM, VM, VM],
        out_specs=[VM] * 4,
        scratch_shapes=[
            pltpu.VMEM((896, C2), BF16),
            pltpu.VMEM((C2, 3 * C2), BF16),
            pltpu.VMEM((C2, C2), BF16),
            pltpu.VMEM((QUAD, QUAD), BF16),
            pltpu.VMEM((CTOK, C2), BF16),
            pltpu.VMEM((CTOK, C2), BF16),
            pltpu.VMEM((CTOK, 3 * C2), BF16),
            pltpu.VMEM((CTOK, C2), BF16),
            pltpu.VMEM((CTOK, C2), BF16),
            pltpu.SemaphoreType.DMA((6,)),
        ],
        compiler_params=pltpu.CompilerParams(vmem_limit_bytes=56 << 20),
        name="section_two",
    )(
        coarse, r_r, r_c, r_x, w_qkv2, w_out2, flag, gain_attn2.reshape(1, -1),
        jnp.asarray(coarse_source()), jnp.asarray(result_source()),
    )
    r_r = shift(s_r, "lat", False)
    r_c = shift(s_c, "lon", False)
    r_x = shift(s_x, ("lat", "lon"), False)
    out = pl.pallas_call(
        join,
        out_shape=sds((CTOK, C2), BF16),
        in_specs=[VM] * 5,
        out_specs=VM,
        compiler_params=pltpu.CompilerParams(vmem_limit_bytes=32 << 20),
        name="join",
    )(main, r_r, r_c, r_x, jnp.asarray(rim_source()))
    return out.reshape(CROWS, CCOLS, C2)


def solution(mesh):
    in_specs = (P("lat", "lon", None),) + (P(),) * 11
    return jax.shard_map(
        on_device, mesh=mesh, in_specs=in_specs, out_specs=P("lat", "lon", None), check_vma=False
    )
```

```python
import functools

import jax
import jax.numpy as jnp
import numpy as np
from jax import lax
from jax.experimental import pallas as pl
from jax.experimental.pallas import tpu as pltpu
from jax.sharding import PartitionSpec as P

HEAD_DIM = 64
WIN = 8
HALF = 4
TOK = WIN * WIN
NB = 2
QUAD = 4 * HEAD_DIM
ROWS, COLS, C1 = 64, 48, 512
MLP1 = 2048
C2 = 1024
CROWS, CCOLS = ROWS // 2, COLS // 2
BANDS, BWIN = ROWS // WIN, COLS // WIN
BTOK = WIN * COLS
CTOK = CROWS * CCOLS
CBANDS, CBWIN = CROWS // WIN, CCOLS // WIN
SCALE = HEAD_DIM**-0.5 * 1.4426950408889634
F32 = jnp.float32
BF16 = jnp.bfloat16


def band_source():
    out = np.zeros((BTOK, 1), np.int32)
    for o in range(BTOK):
        w, t = divmod(o, TOK)
        r = 2 * ((t >> 2) & 3) + ((t >> 4) & 1)
        c = WIN * w + 2 * (t & 3) + (t >> 5) + HALF
        out[o] = r * COLS + c if c < COLS else BTOK + r * HALF + c - COLS
    return out


def coarse_place(r, c):
    return ((r // 4) * BWIN + c // 4) * 16 + (r % 4) * 4 + c % 4


def coarse_send_source():
    out = np.full((128, 1), -1, np.int32)
    for i in range(2 * CCOLS):
        out[i] = coarse_place(i // CCOLS, i % CCOLS)
    for i in range(2 * CROWS):
        out[48 + i] = coarse_place(i // 2, i % 2)
    for i in range(4):
        out[112 + i] = coarse_place(i // 2, i % 2)
    return out


def coarse_source():
    out = np.zeros((CTOK, 1), np.int32)
    for o in range(CTOK):
        w, t = divmod(o, TOK)
        r = WIN * (w // CBWIN) + t // WIN + 2
        c = WIN * (w % CBWIN) + t % WIN + 2
        if r < CROWS and c < CCOLS:
            out[o] = coarse_place(r, c)
        elif c < CCOLS:
            out[o] = CTOK + (r - CROWS) * CCOLS + c
        elif r < CROWS:
            out[o] = CTOK + 48 + r * 2 + c - CCOLS
        else:
            out[o] = CTOK + 112 + (r - CROWS) * 2 + c - CCOLS
    return out


def window_place(r, c):
    return ((r // WIN) * CBWIN + c // WIN) * TOK + (r % WIN) * WIN + c % WIN


def result_source():
    out = np.full((976, 1), -1, np.int32)
    for r in range(HALF, CROWS):
        for c in range(HALF, CCOLS):
            out[r * CCOLS + c] = window_place(r - HALF, c - HALF)
    at = CTOK
    for r in range(CROWS - HALF, CROWS):
        for c in range(CCOLS - HALF):
            out[at] = window_place(r, c)
            at += 1
    for r in range(CROWS - HALF):
        for c in range(CCOLS - HALF, CCOLS):
            out[at] = window_place(r, c)
            at += 1
    for r in range(CROWS - HALF, CROWS):
        for c in range(CCOLS - HALF, CCOLS):
            out[at] = window_place(r, c)
            at += 1
    return out


def rim_source():
    out = np.full((CTOK, 1), -1, np.int32)
    for r in range(CROWS):
        for c in range(CCOLS):
            if r < HALF and c >= HALF:
                out[r * CCOLS + c] = r * (CCOLS - HALF) + c - HALF
            elif r >= HALF and c < HALF:
                out[r * CCOLS + c] = 80 + (r - HALF) * HALF + c
            elif r < HALF:
                out[r * CCOLS + c] = 192 + r * HALF + c
    return out


def picks(source, width):
    lanes = lax.broadcasted_iota(jnp.int32, (source.shape[0], width), 1)
    return (lanes == source).astype(F32).astype(BF16)


def layer_norm(values, scales):
    average = jnp.mean(values, axis=-1, keepdims=True)
    centred = values - average
    spread = jnp.mean(centred * centred, axis=-1, keepdims=True)
    return centred * lax.rsqrt(spread + 1e-05) * scales


def gelu(x):
    return 0.5 * x * (1.0 + jnp.tanh(x * (0.7978845608028654 + 0.035677408136300125 * (x * x))))


def dot(a, b):
    return jnp.dot(a, b, preferred_element_type=F32)


def head_blocks():
    rows = lax.broadcasted_iota(jnp.int32, (QUAD, QUAD), 0) // HEAD_DIM
    lanes = lax.broadcasted_iota(jnp.int32, (QUAD, QUAD), 1) // HEAD_DIM
    return (rows == lanes).astype(F32).astype(BF16)


def segment_max(scores):
    low = lax.broadcasted_iota(jnp.int32, (scores.shape[0], 128), 1) < HEAD_DIM
    out = []
    for t in range(0, QUAD, 128):
        part = scores[:, t : t + 128]
        first = jnp.max(jnp.where(low, part, -3e38), axis=1, keepdims=True)
        second = jnp.max(jnp.where(low, -3e38, part), axis=1, keepdims=True)
        out.append(jnp.where(low, first, second))
    return jnp.concatenate(out, axis=1)


def attend(units, blocks):
    scores = []
    for queries, keys_in, _, bias in units:
        spread = jnp.concatenate([keys_in] * 4, axis=0) * blocks
        score = lax.dot_general(queries, spread, (((1,), (1,)), ((), ())), preferred_element_type=F32) * SCALE
        scores.append(score if bias is None else score + bias)
    weights = [jnp.exp2(score - segment_max(score)).astype(BF16) for score in scores]
    totals = dot(jnp.concatenate(weights, axis=0), blocks)
    mixed = []
    for i, (_, _, values_in, _) in enumerate(units):
        out = dot(weights[i], jnp.concatenate([values_in] * 4, axis=0) * blocks)
        mixed.append((out * (1.0 / totals[i * TOK : i * TOK + TOK])).astype(BF16))
    return mixed


def section_one(
    x_hbm, hr_hbm, he_hbm, hx_hbm, wqkv_hbm, wout_hbm, wup_hbm, wdown_hbm, wmerge_hbm,
    flag, gain_attn, gain_mlp, gain_merge, source, send_source,
    coarse, send_rows, send_cols, send_corner,
    xs, hcs, wqkv, wout, wup, wdown, wmerge, perm, blocks, qkv, attended, merged, sems,
):
    band = pl.program_id(0)
    pairs = (
        (x_hbm, xs.at[0:ROWS]), (hr_hbm, xs.at[ROWS : ROWS + HALF]), (he_hbm, hcs.at[0:240]), (hx_hbm, hcs.at[240:256]),
        (wqkv_hbm, wqkv), (wout_hbm, wout), (wup_hbm, wup), (wdown_hbm, wdown), (wmerge_hbm, wmerge),
    )
    copies = [pltpu.make_async_copy(a, b, sems.at[i]) for i, (a, b) in enumerate(pairs)]

    @pl.when(band == 0)
    def _():
        for c in copies:
            c.start()
        perm[...] = picks(source[...], BTOK + 32)
        blocks[...] = head_blocks()
        for c in copies[:4]:
            c.wait()

    def first(n):
        @pl.when(band == 0)
        def _():
            copies[n].wait()

    tokens = []
    for i in range(NB):
        top = (band * NB + i) * WIN + HALF
        raw = xs[pl.ds(top, WIN)].reshape(BTOK, C1)
        rim = hcs[pl.ds(pl.multiple_of((band * NB + i) * 32, 32), 32)]
        tokens.append(dot(perm[...], jnp.concatenate([raw, rim], axis=0)))
    tokens = jnp.concatenate(tokens, axis=0)
    normed = layer_norm(tokens, gain_attn[...]).astype(BF16)
    first(4)
    for n in range(0, 3 * C1, 512):
        qkv[:, n : n + 512] = dot(normed, wqkv[:, n : n + 512]).astype(BF16)
    half_of = lambda axis: (lax.broadcasted_iota(jnp.int32, (TOK, QUAD), axis) >> 3) & 1
    cut = jnp.where((flag[0] == 1) & (band == BANDS // NB - 1), -1e30, 0.0)
    bias = (half_of(0) != half_of(1)).astype(F32) * cut
    for i in range(NB):
        places = [(i * BWIN + w, g * QUAD) for w in range(BWIN) for g in range(C1 // QUAD)]
        units = [
            [qkv[w * TOK : w * TOK + TOK, k * C1 + g : k * C1 + g + QUAD] for k in range(3)] + [bias if i == NB - 1 else None]
            for w, g in places
        ]
        for (w, g), mixed in zip(places, attend(units, blocks[...])):
            attended[w * TOK : w * TOK + TOK, g : g + QUAD] = mixed
    first(5)
    hidden = (tokens + dot(attended[...], wout[...])).astype(BF16).astype(F32)
    normed = layer_norm(hidden, gain_mlp[...]).astype(BF16)
    first(6)
    first(7)
    total = hidden
    ahead = dot(normed, wup[:, 0:512])
    for n in range(0, MLP1, 512):
        inner = ahead
        if n + 512 < MLP1:
            ahead = dot(normed, wup[:, n + 512 : n + 1024])
        total = total + dot(gelu(inner).astype(BF16), wdown[n : n + 512, :])
    refined = total.astype(BF16).astype(F32).reshape(NB * BWIN, 4, 16, C1)
    quads = jnp.concatenate([refined[:, i] for i in range(4)], axis=-1).reshape(NB * BTOK // 4, 4 * C1)
    rows = NB * BTOK // 4
    merged[pl.ds(pl.multiple_of(band * rows, rows), rows), :] = layer_norm(quads, gain_merge[...]).astype(BF16)

    @pl.when(band == BANDS // NB - 1)
    def _():
        copies[8].wait()
        for n in range(0, C2, 256):
            coarse[:, n : n + 256] = dot(merged[...], wmerge[:, n : n + 256]).astype(BF16)
        sent = dot(picks(send_source[...], CTOK), coarse[...]).astype(BF16)
        send_rows[...] = sent[0:48]
        send_cols[...] = sent[48:112]
        send_corner[...] = sent[112:128]


def section_two(
    own_hbm, hr_hbm, hc_hbm, hx_hbm, wqkv_hbm, wout_hbm, flag, gain, source, out_source,
    main, send_rows, send_cols, send_corner,
    ext, wqkv, wout, blocks, held, normed, qkv, attended, result, sems,
):
    pairs = (
        (own_hbm, ext.at[0:CTOK]), (hr_hbm, ext.at[768:816]), (hc_hbm, ext.at[816:880]), (hx_hbm, ext.at[880:896]),
        (wqkv_hbm, wqkv), (wout_hbm, wout),
    )
    copies = [pltpu.make_async_copy(a, b, sems.at[i]) for i, (a, b) in enumerate(pairs)]
    for c in copies:
        c.start()
    blocks[...] = head_blocks()
    for c in copies[:4]:
        c.wait()
    for i in range(CBANDS):
        here = slice(i * 192, i * 192 + 192)
        tokens = dot(picks(source[here], 896), ext[...])
        held[here] = tokens.astype(BF16)
        normed[here] = layer_norm(tokens, gain[...]).astype(BF16)
    copies[4].wait()
    for n in range(0, 3 * C2, 512):
        qkv[:, n : n + 512] = dot(normed[...], wqkv[:, n : n + 512]).astype(BF16)

    half_of = lambda axis: (lax.broadcasted_iota(jnp.int32, (TOK, QUAD), axis) >> 5) & 1

    def one_band(i, carry):
        cut = jnp.where((flag[0] == 1) & (i == CBANDS - 1), -1e30, 0.0)
        bias = (half_of(0) != half_of(1)).astype(F32) * cut
        here = pl.ds(pl.multiple_of(i * 192, 192), 192)
        places = [(slice(w * TOK, w * TOK + TOK), g * QUAD) for w in range(CBWIN) for g in range(C2 // QUAD)]
        band = [qkv[here, k * C2 : k * C2 + C2] for k in range(3)]
        units = [[part[w, g : g + QUAD] for part in band] + [bias] for w, g in places]
        mixed = attend(units, blocks[...])
        for w in range(CBWIN):
            row = jnp.concatenate(mixed[w * 4 : w * 4 + 4], axis=1)
            attended[pl.ds(pl.multiple_of(i * 192 + w * TOK, TOK), TOK), :] = row
        return carry

    lax.fori_loop(0, CBANDS, one_band, 0)
    copies[5].wait()
    for n in range(0, C2, 256):
        here = slice(n, n + 256)
        result[:, here] = (held[:, here].astype(F32) + dot(attended[...], wout[:, here])).astype(BF16)
    for i in range(CBANDS):
        here = slice(i * 192, i * 192 + 192)
        main[here] = dot(picks(out_source[here], CTOK), result[...]).astype(BF16)
    sent = dot(picks(out_source[CTOK:], CTOK), result[...]).astype(BF16)
    send_rows[...] = sent[0:80]
    send_cols[...] = sent[80:192]
    send_corner[...] = sent[192:208]


def join(main, rows, cols, corner, source, out):
    rim = jnp.concatenate([rows[...], cols[...], corner[...]], axis=0)
    out[...] = (main[...].astype(F32) + dot(picks(source[...], 208), rim)).astype(BF16)


ANY = pl.BlockSpec(memory_space=pl.ANY)
VM = pl.BlockSpec(memory_space=pltpu.VMEM)
SM = pl.BlockSpec(memory_space=pltpu.SMEM)


def whole(shape):
    return pl.BlockSpec(shape, lambda b: (0,) * len(shape))


def shift(values, axes, back):
    if isinstance(axes, str):
        count = lax.axis_size(axes)
        pairs = [(i, (i + 1) % count) for i in range(count)]
    else:
        lat, lon = (lax.axis_size(a) for a in axes)
        pairs = [(i * lon + j, ((i + 1) % lat) * lon + (j + 1) % lon) for i in range(lat) for j in range(lon)]
    if back:
        pairs = [(b, a) for a, b in pairs]
    return lax.ppermute(values, axes, pairs)


def on_device(
    tokens, gain_attn1, w_qkv1, w_out1, gain_mlp1, w_up, w_down, gain_merge, w_merge, gain_attn2, w_qkv2, w_out2,
):
    flag = (lax.axis_index("lat") == lax.axis_size("lat") - 1).astype(jnp.int32).reshape(1)
    rim_r = shift(tokens[0:HALF], "lat", True)
    rim_c = shift(tokens[HALF:, 0:HALF].reshape(240, C1), "lon", True)
    rim_x = shift(tokens[0:HALF, 0:HALF].reshape(16, C1), ("lat", "lon"), True)
    sds = jax.ShapeDtypeStruct
    coarse, s_r, s_c, s_x = pl.pallas_call(
        section_one,
        grid=(BANDS // NB,),
        out_shape=[sds((CTOK, C2), BF16), sds((48, C2), BF16), sds((64, C2), BF16), sds((16, C2), BF16)],
        in_specs=[ANY] * 9 + [SM, whole((1, C1)), whole((1, C1)), whole((1, 4 * C1)), whole((BTOK, 1)), whole((128, 1))],
        out_specs=[whole((CTOK, C2)), whole((48, C2)), whole((64, C2)), whole((16, C2))],
        scratch_shapes=[
            pltpu.VMEM((ROWS + HALF, COLS, C1), BF16),
            pltpu.VMEM((256, C1), BF16),
            pltpu.VMEM((C1, 3 * C1), BF16),
            pltpu.VMEM((C1, C1), BF16),
            pltpu.VMEM((C1, MLP1), BF16),
            pltpu.VMEM((MLP1, C1), BF16),
            pltpu.VMEM((4 * C1, C2), BF16),
            pltpu.VMEM((BTOK, BTOK + 32), BF16),
            pltpu.VMEM((QUAD, QUAD), BF16),
            pltpu.VMEM((NB * BTOK, 3 * C1), BF16),
            pltpu.VMEM((NB * BTOK, C1), BF16),
            pltpu.VMEM((CTOK, 4 * C1), BF16),
            pltpu.SemaphoreType.DMA((9,)),
        ],
        compiler_params=pltpu.CompilerParams(vmem_limit_bytes=56 << 20),
        name="section_one",
    )(
        tokens, rim_r, rim_c, rim_x, w_qkv1, w_out1, w_up, w_down, w_merge,
        flag, gain_attn1.reshape(1, -1), gain_mlp1.reshape(1, -1), gain_merge.reshape(1, -1),
        jnp.asarray(band_source()), jnp.asarray(coarse_send_source()),
    )
    r_r = shift(s_r, "lat", True)
    r_c = shift(s_c, "lon", True)
    r_x = shift(s_x, ("lat", "lon"), True)
    main, s_r, s_c, s_x = pl.pallas_call(
        section_two,
        out_shape=[sds((CTOK, C2), BF16), sds((80, C2), BF16), sds((112, C2), BF16), sds((16, C2), BF16)],
        in_specs=[ANY] * 6 + [SM, VM, VM, VM],
        out_specs=[VM] * 4,
        scratch_shapes=[
            pltpu.VMEM((896, C2), BF16),
            pltpu.VMEM((C2, 3 * C2), BF16),
            pltpu.VMEM((C2, C2), BF16),
            pltpu.VMEM((QUAD, QUAD), BF16),
            pltpu.VMEM((CTOK, C2), BF16),
            pltpu.VMEM((CTOK, C2), BF16),
            pltpu.VMEM((CTOK, 3 * C2), BF16),
            pltpu.VMEM((CTOK, C2), BF16),
            pltpu.VMEM((CTOK, C2), BF16),
            pltpu.SemaphoreType.DMA((6,)),
        ],
        compiler_params=pltpu.CompilerParams(vmem_limit_bytes=56 << 20),
        name="section_two",
    )(
        coarse, r_r, r_c, r_x, w_qkv2, w_out2, flag, gain_attn2.reshape(1, -1),
        jnp.asarray(coarse_source()), jnp.asarray(result_source()),
    )
    r_r = shift(s_r, "lat", False)
    r_c = shift(s_c, "lon", False)
    r_x = shift(s_x, ("lat", "lon"), False)
    out = pl.pallas_call(
        join,
        out_shape=sds((CTOK, C2), BF16),
        in_specs=[VM] * 5,
        out_specs=VM,
        compiler_params=pltpu.CompilerParams(vmem_limit_bytes=32 << 20),
        name="join",
    )(main, r_r, r_c, r_x, jnp.asarray(rim_source()))
    return out.reshape(CROWS, CCOLS, C2)


def solution(mesh):
    in_specs = (P("lat", "lon", None),) + (P(),) * 11
    return jax.shard_map(
        on_device, mesh=mesh, in_specs=in_specs, out_specs=P("lat", "lon", None), check_vma=False
    )
```

```python
import functools

import jax
import jax.numpy as jnp
import numpy as np
from jax import lax
from jax.experimental import pallas as pl
from jax.experimental.pallas import tpu as pltpu
from jax.sharding import PartitionSpec as P

HEAD_DIM = 64
WIN = 8
HALF = 4
TOK = WIN * WIN
NB = 2
QUAD = 4 * HEAD_DIM
ROWS, COLS, C1 = 64, 48, 512
MLP1 = 2048
C2 = 1024
CROWS, CCOLS = ROWS // 2, COLS // 2
BANDS, BWIN = ROWS // WIN, COLS // WIN
BTOK = WIN * COLS
CTOK = CROWS * CCOLS
STEPS = BANDS // NB
ORDER = "FBBFBFFFBFFBFFFBFBF"
CBANDS, CBWIN = CROWS // WIN, CCOLS // WIN
SCALE = HEAD_DIM**-0.5 * 1.4426950408889634
F32 = jnp.float32
BF16 = jnp.bfloat16


def band_source():
    out = np.zeros((BTOK, 1), np.int32)
    for o in range(BTOK):
        w, t = divmod(o, TOK)
        r = 2 * ((t >> 2) & 3) + ((t >> 4) & 1)
        c = WIN * w + 2 * (t & 3) + (t >> 5) + HALF
        out[o] = r * COLS + c if c < COLS else BTOK + r * HALF + c - COLS
    return out


def coarse_place(r, c):
    return ((r // 4) * BWIN + c // 4) * 16 + (r % 4) * 4 + c % 4


def coarse_send_source():
    out = np.full((128, 1), -1, np.int32)
    for i in range(2 * CCOLS):
        out[i] = coarse_place(i // CCOLS, i % CCOLS)
    for i in range(2 * CROWS):
        out[48 + i] = coarse_place(i // 2, i % 2)
    for i in range(4):
        out[112 + i] = coarse_place(i // 2, i % 2)
    return out


def coarse_source():
    out = np.zeros((CTOK, 1), np.int32)
    for o in range(CTOK):
        w, t = divmod(o, TOK)
        r = WIN * (w // CBWIN) + t // WIN + 2
        c = WIN * (w % CBWIN) + t % WIN + 2
        if r < CROWS and c < CCOLS:
            out[o] = coarse_place(r, c)
        elif c < CCOLS:
            out[o] = CTOK + (r - CROWS) * CCOLS + c
        elif r < CROWS:
            out[o] = CTOK + 48 + r * 2 + c - CCOLS
        else:
            out[o] = CTOK + 112 + (r - CROWS) * 2 + c - CCOLS
    return out


def window_place(r, c):
    return ((r // WIN) * CBWIN + c // WIN) * TOK + (r % WIN) * WIN + c % WIN


def result_source():
    out = np.full((976, 1), -1, np.int32)
    for r in range(HALF, CROWS):
        for c in range(HALF, CCOLS):
            out[r * CCOLS + c] = window_place(r - HALF, c - HALF)
    at = CTOK
    for r in range(CROWS - HALF, CROWS):
        for c in range(CCOLS - HALF):
            out[at] = window_place(r, c)
            at += 1
    for r in range(CROWS - HALF):
        for c in range(CCOLS - HALF, CCOLS):
            out[at] = window_place(r, c)
            at += 1
    for r in range(CROWS - HALF, CROWS):
        for c in range(CCOLS - HALF, CCOLS):
            out[at] = window_place(r, c)
            at += 1
    return out


def rim_source():
    out = np.full((CTOK, 1), -1, np.int32)
    for r in range(CROWS):
        for c in range(CCOLS):
            if r < HALF and c >= HALF:
                out[r * CCOLS + c] = r * (CCOLS - HALF) + c - HALF
            elif r >= HALF and c < HALF:
                out[r * CCOLS + c] = 80 + (r - HALF) * HALF + c
            elif r < HALF:
                out[r * CCOLS + c] = 192 + r * HALF + c
    return out


def picks(source, width):
    lanes = lax.broadcasted_iota(jnp.int32, (source.shape[0], width), 1)
    return (lanes == source).astype(F32).astype(BF16)


def layer_norm(values, scales):
    average = jnp.mean(values, axis=-1, keepdims=True)
    centred = values - average
    spread = jnp.mean(centred * centred, axis=-1, keepdims=True)
    return centred * lax.rsqrt(spread + 1e-05) * scales


def gelu(x):
    return 0.5 * x * (1.0 + jnp.tanh(x * (0.7978845608028654 + 0.035677408136300125 * (x * x))))


def dot(a, b):
    return jnp.dot(a, b, preferred_element_type=F32)


def head_blocks():
    rows = lax.broadcasted_iota(jnp.int32, (QUAD, QUAD), 0) // HEAD_DIM
    lanes = lax.broadcasted_iota(jnp.int32, (QUAD, QUAD), 1) // HEAD_DIM
    return (rows == lanes).astype(F32).astype(BF16)


def segment_max(scores):
    low = lax.broadcasted_iota(jnp.int32, (scores.shape[0], 128), 1) < HEAD_DIM
    out = []
    for t in range(0, QUAD, 128):
        part = scores[:, t : t + 128]
        first = jnp.max(jnp.where(low, part, -3e38), axis=1, keepdims=True)
        second = jnp.max(jnp.where(low, -3e38, part), axis=1, keepdims=True)
        out.append(jnp.where(low, first, second))
    return jnp.concatenate(out, axis=1)


def attend_scores(units, blocks):
    scores = []
    for queries, keys_in, _, bias in units:
        spread = jnp.concatenate([keys_in] * 4, axis=0) * blocks
        score = lax.dot_general(queries, spread, (((1,), (1,)), ((), ())), preferred_element_type=F32) * SCALE
        scores.append(score if bias is None else score + bias)
    return scores


def attend_weights(scores):
    return [jnp.exp2(score - segment_max(score)).astype(BF16) for score in scores]


def attend_values(units, weights, blocks):
    totals = dot(jnp.concatenate(weights, axis=0), blocks)
    mixed = []
    for i, (_, _, values_in, _) in enumerate(units):
        out = dot(weights[i], jnp.concatenate([values_in] * 4, axis=0) * blocks)
        mixed.append((out * (1.0 / totals[i * TOK : i * TOK + TOK])).astype(BF16))
    return mixed


def drive(first, second, order):
    streams = {"F": first, "B": second}
    for name in order:
        next(streams[name])
    for stream in (first, second):
        for _ in stream:
            pass


def section_one(
    x_hbm, wqkv_hbm, wout_hbm, wup_hbm, wdown_hbm, wmerge_hbm,
    rim_rows, rim_cols, rim_corner, flag, gain_attn, gain_mlp, gain_merge, source, send_source,
    coarse, send_rows, send_cols, send_corner,
    xs, hcs, wqkv, wout, wup, wdown, wmerge, perm, blocks, qkv, attended, held, merged, sems,
):
    step = pl.program_id(0)
    head = NB * WIN + HALF
    pairs = (
        (x_hbm.at[0:head], xs.at[0:head]), (wqkv_hbm, wqkv), (x_hbm.at[head:ROWS], xs.at[head:ROWS]),
        (wout_hbm, wout), (wup_hbm, wup), (wdown_hbm, wdown), (wmerge_hbm, wmerge),
    )
    copies = [pltpu.make_async_copy(a, b, sems.at[i]) for i, (a, b) in enumerate(pairs)]

    def front(opening):
        if opening:
            copies[0].wait()
        tokens = []
        for i in range(NB):
            top = (step * NB + i) * WIN + HALF
            raw = xs[pl.ds(top, WIN)].reshape(BTOK, C1)
            rim = hcs[pl.ds(pl.multiple_of((step * NB + i) * 32, 32), 32)]
            tokens.append(dot(perm[...], jnp.concatenate([raw, rim], axis=0)))
        tokens = jnp.concatenate(tokens, axis=0)
        yield
        normed = layer_norm(tokens, gain_attn[...]).astype(BF16)
        if opening:
            copies[1].wait()
        yield
        for n in range(0, 3 * C1, 512):
            qkv[:, n : n + 512] = dot(normed, wqkv[:, n : n + 512]).astype(BF16)
            yield
        half_of = lambda axis: (lax.broadcasted_iota(jnp.int32, (TOK, QUAD), axis) >> 3) & 1
        cut = jnp.where((flag[0] == 1) & (step == STEPS - 1), -1e30, 0.0)
        bias = (half_of(0) != half_of(1)).astype(F32) * cut
        for i in range(NB):
            places = [(i * BWIN + w, g * QUAD) for w in range(BWIN) for g in range(C1 // QUAD)]
            units = [
                [qkv[w * TOK : w * TOK + TOK, k * C1 + g : k * C1 + g + QUAD] for k in range(3)]
                + [bias if i == NB - 1 and not opening else None]
                for w, g in places
            ]
            scores = attend_scores(units, blocks[...])
            yield
            weights = attend_weights(scores)
            yield
            for (w, g), mixed in zip(places, attend_values(units, weights, blocks[...])):
                attended[w * TOK : w * TOK + TOK, g : g + QUAD] = mixed
            yield
        if opening:
            copies[3].wait()
        held[...] = (tokens + dot(attended[...], wout[...])).astype(BF16)
        if opening:
            for c in (2, 4, 5):
                copies[c].wait()
        yield

    def back():
        hidden = held[...].astype(F32)
        normed = layer_norm(hidden, gain_mlp[...]).astype(BF16)
        yield
        total = hidden
        ahead = dot(normed, wup[:, 0:512])
        yield
        for n in range(0, MLP1, 512):
            inner = ahead
            if n + 512 < MLP1:
                ahead = dot(normed, wup[:, n + 512 : n + 1024])
            total = total + dot(gelu(inner).astype(BF16), wdown[n : n + 512, :])
            yield
        refined = total.astype(BF16).astype(F32).reshape(NB * BWIN, 4, 16, C1)
        quads = jnp.concatenate([refined[:, i] for i in range(4)], axis=-1).reshape(NB * BTOK // 4, 4 * C1)
        rows = NB * BTOK // 4
        merged[pl.ds(pl.multiple_of((step - 1) * rows, rows), rows), :] = layer_norm(quads, gain_merge[...]).astype(BF16)
        yield

    @pl.when(step == 0)
    def _():
        for c in copies:
            c.start()
        perm[...] = picks(source[...], BTOK + 32)
        blocks[...] = head_blocks()
        xs[ROWS : ROWS + HALF] = rim_rows[...]
        hcs[0:240] = rim_cols[16:256]
        hcs[240:256] = rim_corner[...]
        drive(front(True), iter(()), "")

    @pl.when((step > 0) & (step < STEPS))
    def _():
        drive(front(False), back(), ORDER)

    @pl.when(step == STEPS)
    def _():
        drive(iter(()), back(), "")
        copies[6].wait()
        for n in range(0, C2, 256):
            coarse[:, n : n + 256] = dot(merged[...], wmerge[:, n : n + 256]).astype(BF16)
        sent = dot(picks(send_source[...], CTOK), coarse[...]).astype(BF16)
        send_rows[...] = sent[0:48]
        send_cols[...] = sent[48:112]
        send_corner[...] = sent[112:128]


def section_two(
    wqkv_hbm, wout_hbm, own, rim_rows, rim_cols, rim_corner, flag, gain, source, send_source,
    result, send_rows, send_cols, send_corner,
    wqkv, wout, blocks, held, normed, qkv, attended, sems,
):
    groups = C2 // QUAD
    copies = []
    for g in range(groups):
        for k in range(3):
            here = slice(k * C2 + g * QUAD, k * C2 + g * QUAD + QUAD)
            copies.append(pltpu.make_async_copy(wqkv_hbm.at[:, here], wqkv.at[:, here], sems.at[g * 3 + k]))
    copies.append(pltpu.make_async_copy(wout_hbm, wout, sems.at[3 * groups]))
    for c in copies:
        c.start()
    blocks[...] = head_blocks()
    rim = jnp.concatenate([rim_rows[...], rim_cols[...], rim_corner[...]], axis=0)
    for i in range(CBANDS):
        here = slice(i * 192, i * 192 + 192)
        low, high = i * 192, min(i * 192 + 288, CTOK)
        tokens = dot(picks(source[here] - low, high - low), own[low:high]) + dot(picks(source[here] - CTOK, 128), rim)
        held[here] = tokens.astype(BF16)
        normed[here] = layer_norm(tokens, gain[...]).astype(BF16)
    half_of = lambda axis: (lax.broadcasted_iota(jnp.int32, (TOK, QUAD), axis) >> 5) & 1
    bias = (half_of(0) != half_of(1)).astype(F32) * jnp.where(flag[0] == 1, -1e30, 0.0)

    def project(g):
        for k in range(3):
            here = slice(k * C2 + g * QUAD, k * C2 + g * QUAD + QUAD)
            qkv[:, here] = dot(normed[...], wqkv[:, here]).astype(BF16)

    for c in copies[:3]:
        c.wait()
    project(0)
    for c in copies[3:]:
        c.wait()
    for g in range(groups):
        units = [
            [qkv[w * TOK : w * TOK + TOK, k * C2 + g * QUAD : k * C2 + g * QUAD + QUAD] for k in range(3)]
            + [bias if w >= CBWIN * (CBANDS - 1) else None]
            for w in range(CBWIN * CBANDS)
        ]
        scores = attend_scores(units, blocks[...])
        if g + 1 < groups:
            project(g + 1)
        weights = attend_weights(scores)
        for w, mixed in enumerate(attend_values(units, weights, blocks[...])):
            attended[w * TOK : w * TOK + TOK, g * QUAD : g * QUAD + QUAD] = mixed
    for n in range(0, C2, 256):
        here = slice(n, n + 256)
        result[:, here] = (held[:, here].astype(F32) + dot(attended[...], wout[:, here])).astype(BF16)
    sent = dot(picks(send_source[...], CTOK), result[...]).astype(BF16)
    send_rows[...] = sent[0:80]
    send_cols[...] = sent[80:192]
    send_corner[...] = sent[192:208]


def place(result, source, main):
    for i in range(CBANDS):
        here = slice(i * 192, i * 192 + 192)
        low = max(i - 1, 0) * 192
        main[here] = dot(picks(source[here] - low, here.stop - low), result[low : here.stop]).astype(BF16)


def join(main, rows, cols, corner, source, out):
    rim = jnp.concatenate([rows[...], cols[...], corner[...]], axis=0)
    out[...] = (main[...].astype(F32) + dot(picks(source[...], 208), rim)).astype(BF16)


HBM = pl.BlockSpec(memory_space=pltpu.HBM)
VM = pl.BlockSpec(memory_space=pltpu.VMEM)
SM = pl.BlockSpec(memory_space=pltpu.SMEM)


def whole(shape):
    return pl.BlockSpec(shape, lambda b: (0,) * len(shape))


def shift(values, axes, back):
    if isinstance(axes, str):
        count = lax.axis_size(axes)
        pairs = [(i, (i + 1) % count) for i in range(count)]
    else:
        lat, lon = (lax.axis_size(a) for a in axes)
        pairs = [(i * lon + j, ((i + 1) % lat) * lon + (j + 1) % lon) for i in range(lat) for j in range(lon)]
    if back:
        pairs = [(b, a) for a, b in pairs]
    return lax.ppermute(values, axes, pairs)


def sds(*shape):
    return jax.ShapeDtypeStruct(shape, BF16)


def run_one(tokens, w_qkv, w_out, w_up, w_down, w_merge, rim_r, rim_c, rim_x, flag, gain_attn, gain_mlp, gain_merge):
    return pl.pallas_call(
        section_one,
        grid=(STEPS + 1,),
        out_shape=[sds(CTOK, C2), sds(48, C2), sds(64, C2), sds(16, C2)],
        in_specs=[HBM] * 6 + [VM] * 3
        + [SM, whole((1, C1)), whole((1, C1)), whole((1, 4 * C1)), whole((BTOK, 1)), whole((128, 1))],
        out_specs=[VM] * 4,
        scratch_shapes=[
            pltpu.VMEM((ROWS + HALF, COLS, C1), BF16),
            pltpu.VMEM((256, C1), BF16),
            pltpu.VMEM((C1, 3 * C1), BF16),
            pltpu.VMEM((C1, C1), BF16),
            pltpu.VMEM((C1, MLP1), BF16),
            pltpu.VMEM((MLP1, C1), BF16),
            pltpu.VMEM((4 * C1, C2), BF16),
            pltpu.VMEM((BTOK, BTOK + 32), BF16),
            pltpu.VMEM((QUAD, QUAD), BF16),
            pltpu.VMEM((NB * BTOK, 3 * C1), BF16),
            pltpu.VMEM((NB * BTOK, C1), BF16),
            pltpu.VMEM((NB * BTOK, C1), BF16),
            pltpu.VMEM((CTOK, 4 * C1), BF16),
            pltpu.SemaphoreType.DMA((7,)),
        ],
        compiler_params=pltpu.CompilerParams(vmem_limit_bytes=48 << 20),
        name="section_one",
    )(
        tokens, w_qkv, w_out, w_up, w_down, w_merge, rim_r, rim_c, rim_x,
        flag, gain_attn.reshape(1, -1), gain_mlp.reshape(1, -1), gain_merge.reshape(1, -1),
        jnp.asarray(band_source()), jnp.asarray(coarse_send_source()),
    )


def run_two(w_qkv, w_out, coarse, rim_r, rim_c, rim_x, flag, gain):
    return pl.pallas_call(
        section_two,
        grid=(1,),
        out_shape=[sds(CTOK, C2), sds(80, C2), sds(112, C2), sds(16, C2)],
        in_specs=[HBM] * 2 + [VM] * 4 + [SM, whole((1, C2)), whole((CTOK, 1)), whole((208, 1))],
        out_specs=[VM] * 4,
        scratch_shapes=[
            pltpu.VMEM((C2, 3 * C2), BF16),
            pltpu.VMEM((C2, C2), BF16),
            pltpu.VMEM((QUAD, QUAD), BF16),
            pltpu.VMEM((CTOK, C2), BF16),
            pltpu.VMEM((CTOK, C2), BF16),
            pltpu.VMEM((CTOK, 3 * C2), BF16),
            pltpu.VMEM((CTOK, C2), BF16),
            pltpu.SemaphoreType.DMA((13,)),
        ],
        compiler_params=pltpu.CompilerParams(vmem_limit_bytes=48 << 20),
        name="section_two",
    )(
        w_qkv, w_out, coarse, rim_r, rim_c, rim_x, flag, gain.reshape(1, -1),
        jnp.asarray(coarse_source()), jnp.asarray(result_source()[CTOK:]),
    )


def run_place(result):
    return pl.pallas_call(
        place,
        grid=(1,),
        out_shape=sds(CTOK, C2),
        in_specs=[VM, whole((CTOK, 1))],
        out_specs=VM,
        cost_estimate=pl.CostEstimate(flops=2 * CTOK * 384 * C2, bytes_accessed=5 << 20, transcendentals=0),
        compiler_params=pltpu.CompilerParams(vmem_limit_bytes=32 << 20),
        name="place",
    )(result, jnp.asarray(result_source()[:CTOK]))


def run_join(main, rim_r, rim_c, rim_x):
    return pl.pallas_call(
        join,
        grid=(1,),
        out_shape=sds(CTOK, C2),
        in_specs=[VM, VM, VM, VM, whole((CTOK, 1))],
        out_specs=whole((CTOK, C2)),
        compiler_params=pltpu.CompilerParams(vmem_limit_bytes=32 << 20),
        name="join",
    )(main, rim_r, rim_c, rim_x, jnp.asarray(rim_source()))


def on_device(
    tokens, gain_attn1, w_qkv1, w_out1, gain_mlp1, w_up, w_down, gain_merge, w_merge, gain_attn2, w_qkv2, w_out2,
):
    flag = (lax.axis_index("lat") == lax.axis_size("lat") - 1).astype(jnp.int32).reshape(1)
    strip = tokens[:, 0:HALF].reshape(256, C1)
    rim_c = shift(strip, "lon", True)
    rim_r = shift(tokens[0:HALF], "lat", True)
    rim_x = shift(strip[0:16], ("lat", "lon"), True)
    coarse, s_r, s_c, s_x = run_one(
        tokens, w_qkv1, w_out1, w_up, w_down, w_merge, rim_r, rim_c, rim_x, flag, gain_attn1, gain_mlp1, gain_merge
    )
    r_r = shift(s_r, "lat", True)
    r_c = shift(s_c, "lon", True)
    r_x = shift(s_x, ("lat", "lon"), True)
    result, s_r, s_c, s_x = run_two(w_qkv2, w_out2, coarse, r_r, r_c, r_x, flag, gain_attn2)
    r_r = shift(s_r, "lat", False)
    r_c = shift(s_c, "lon", False)
    r_x = shift(s_x, ("lat", "lon"), False)
    return run_join(run_place(result), r_r, r_c, r_x).reshape(CROWS, CCOLS, C2)


def solution(mesh):
    in_specs = (P("lat", "lon", None),) + (P(),) * 11
    return jax.shard_map(
        on_device, mesh=mesh, in_specs=in_specs, out_specs=P("lat", "lon", None), check_vma=False
    )
```

```python
import functools

import jax
import jax.numpy as jnp
import numpy as np
from jax import lax
from jax.experimental import pallas as pl
from jax.experimental.pallas import tpu as pltpu
from jax.sharding import PartitionSpec as P

HEAD_DIM = 64
WIN = 8
HALF = 4
TOK = WIN * WIN
QUAD = 4 * HEAD_DIM
ROWS, COLS, C1 = 64, 48, 512
MLP1 = 2048
C2 = 1024
CROWS, CCOLS = ROWS // 2, COLS // 2
BANDS, BWIN = ROWS // WIN, COLS // WIN
BTOK = WIN * COLS
CTOK = CROWS * CCOLS
INNER = BWIN - 1
EARLY, LATE = 36, 12
GROUPS = ((0, 1), (2, 3), (4, 5), (6,))
ORDER = "FBFBFBBFBFBFBBFBFBFB"
CBANDS, CBWIN = CROWS // WIN, CCOLS // WIN
VMEM_ONE = 56
SCALE = HEAD_DIM**-0.5 * 1.4426950408889634
F32 = jnp.float32
BF16 = jnp.bfloat16


def token_place(t):
    return 2 * ((t >> 2) & 3) + ((t >> 4) & 1), 2 * (t & 3) + (t >> 5) + HALF


def inner_source():
    out = np.zeros((INNER * TOK, 1), np.int32)
    for o in range(INNER * TOK):
        r, c = token_place(o % TOK)
        out[o] = r * COLS + o // TOK * WIN + c
    return out


def last_band_source():
    out = np.zeros((BTOK, 1), np.int32)
    for o in range(BTOK):
        r, c = token_place(o % TOK)
        c += o // TOK * WIN
        out[o] = r * COLS + c if c < COLS else BTOK + r * HALF + c - COLS
    return out


def last_column_source():
    out = np.zeros((TOK, 1), np.int32)
    for o in range(TOK):
        r, c = token_place(o)
        c += WIN
        out[o] = r * 16 + c if c < 16 else 128 + r * HALF + c - 16
    return out


def early_place(band, col):
    if band == BANDS - 1:
        return 23 + col
    if col == INNER:
        return 29 + band
    return INNER * band + col if band < 4 else 20 + band - 4


def coarse_place(r, c):
    return ((r // 4) * BWIN + c // 4) * 16 + (r % 4) * 4 + c % 4


def early_coarse(r, c):
    return early_place(r // 4, c // 4) * 16 + (r % 4) * 4 + c % 4


def coarse_send_source():
    out = np.full((128, 1), -1, np.int32)
    for i in range(2 * CCOLS):
        out[i] = early_coarse(i // CCOLS, i % CCOLS)
    for i in range(2 * CROWS):
        out[48 + i] = early_coarse(i // 2, i % 2)
    for i in range(4):
        out[112 + i] = early_coarse(i // 2, i % 2)
    return out


def coarse_source():
    out = np.zeros((CTOK, 1), np.int32)
    for o in range(CTOK):
        w, t = divmod(o, TOK)
        r = WIN * (w // CBWIN) + t // WIN + 2
        c = WIN * (w % CBWIN) + t % WIN + 2
        if r < CROWS and c < CCOLS:
            out[o] = coarse_place(r, c)
        elif c < CCOLS:
            out[o] = CTOK + (r - CROWS) * CCOLS + c
        elif r < CROWS:
            out[o] = CTOK + 48 + r * 2 + c - CCOLS
        else:
            out[o] = CTOK + 112 + (r - CROWS) * 2 + c - CCOLS
    return out


def window_place(r, c):
    return ((r // WIN) * CBWIN + c // WIN) * TOK + (r % WIN) * WIN + c % WIN


def result_source():
    out = np.full((976, 1), -1, np.int32)
    for r in range(HALF, CROWS):
        for c in range(HALF, CCOLS):
            out[r * CCOLS + c] = window_place(r - HALF, c - HALF)
    at = CTOK
    for r in range(CROWS - HALF, CROWS):
        for c in range(CCOLS - HALF):
            out[at] = window_place(r, c)
            at += 1
    for r in range(CROWS - HALF):
        for c in range(CCOLS - HALF, CCOLS):
            out[at] = window_place(r, c)
            at += 1
    for r in range(CROWS - HALF, CROWS):
        for c in range(CCOLS - HALF, CCOLS):
            out[at] = window_place(r, c)
            at += 1
    return out


def rim_source():
    out = np.full((CTOK, 1), -1, np.int32)
    for r in range(CROWS):
        for c in range(CCOLS):
            if r < HALF and c >= HALF:
                out[r * CCOLS + c] = r * (CCOLS - HALF) + c - HALF
            elif r >= HALF and c < HALF:
                out[r * CCOLS + c] = 80 + (r - HALF) * HALF + c
            elif r < HALF:
                out[r * CCOLS + c] = 192 + r * HALF + c
    return out


def picks(source, width):
    lanes = lax.broadcasted_iota(jnp.int32, (source.shape[0], width), 1)
    return (lanes == source).astype(F32).astype(BF16)


def layer_norm(values, scales):
    average = jnp.mean(values, axis=-1, keepdims=True)
    centred = values - average
    spread = jnp.mean(centred * centred, axis=-1, keepdims=True)
    return centred * lax.rsqrt(spread + 1e-05) * scales


def gelu(x):
    return 0.5 * x * (1.0 + jnp.tanh(x * (0.7978845608028654 + 0.035677408136300125 * (x * x))))


def dot(a, b):
    return jnp.dot(a, b, preferred_element_type=F32)


def head_blocks():
    rows = lax.broadcasted_iota(jnp.int32, (QUAD, QUAD), 0) // HEAD_DIM
    lanes = lax.broadcasted_iota(jnp.int32, (QUAD, QUAD), 1) // HEAD_DIM
    return (rows == lanes).astype(F32).astype(BF16)


def segment_max(scores):
    low = lax.broadcasted_iota(jnp.int32, (scores.shape[0], 128), 1) < HEAD_DIM
    out = []
    for t in range(0, QUAD, 128):
        part = scores[:, t : t + 128]
        first = jnp.max(jnp.where(low, part, -3e38), axis=1, keepdims=True)
        second = jnp.max(jnp.where(low, -3e38, part), axis=1, keepdims=True)
        out.append(jnp.where(low, first, second))
    return jnp.concatenate(out, axis=1)


def attend_scores(units, blocks):
    scores = []
    for queries, keys_in, _, bias in units:
        spread = jnp.concatenate([keys_in] * 4, axis=0) * blocks
        score = lax.dot_general(queries, spread, (((1,), (1,)), ((), ())), preferred_element_type=F32) * SCALE
        scores.append(score if bias is None else score + bias)
    return scores


def attend_weights(scores):
    return [jnp.exp2(score - segment_max(score)).astype(BF16) for score in scores]


def attend_values(units, weights, blocks):
    totals = dot(jnp.concatenate(weights, axis=0), blocks)
    mixed = []
    for i, (_, _, values_in, _) in enumerate(units):
        out = dot(weights[i], jnp.concatenate([values_in] * 4, axis=0) * blocks)
        mixed.append((out * (1.0 / totals[i * TOK : i * TOK + TOK])).astype(BF16))
    return mixed


def drive(first, second, order):
    streams = {"F": first, "B": second}
    for name in order:
        next(streams[name])
    for stream in (first, second):
        for _ in stream:
            pass


def attention_inner(
    x_hbm, wqkv_hbm, wout_hbm, gain, source,
    early, late, xs, wqkv, wout, perm, blocks, qkv, held, attended, sems,
):
    cuts = [0] + [(g[-1] + 1) * WIN + HALF for g in GROUPS]
    pairs = [(x_hbm.at[i:j], xs.at[i:j]) for i, j in zip(cuts, cuts[1:])] + [(wqkv_hbm, wqkv), (wout_hbm, wout)]
    copies = [pltpu.make_async_copy(a, b, sems.at[i]) for i, (a, b) in enumerate(pairs)]
    for i in (0, 4, 1, 5, 2, 3):
        copies[i].start()
    perm[...] = picks(source[...], BTOK)
    blocks[...] = head_blocks()
    size = INNER * TOK

    def project(group):
        here = slice(group[0] * size, group[-1] * size + size)
        tokens = [dot(perm[...], xs[b * WIN + HALF : b * WIN + HALF + WIN].reshape(BTOK, C1)) for b in group]
        tokens = jnp.concatenate(tokens, axis=0)
        held[here] = tokens.astype(BF16)
        normed = layer_norm(tokens, gain[...]).astype(BF16)
        for n in range(0, 3 * C1, 512):
            qkv[here, n : n + 512] = dot(normed, wqkv[:, n : n + 512]).astype(BF16)

    copies[0].wait()
    copies[4].wait()
    project(GROUPS[0])
    for i in (1, 2, 3, 5):
        copies[i].wait()
    for k, group in enumerate(GROUPS):
        first, count = group[0] * INNER, len(group) * INNER
        places = [(w, g * QUAD) for w in range(first, first + count) for g in range(C1 // QUAD)]
        units = [
            [qkv[w * TOK : w * TOK + TOK, k * C1 + g : k * C1 + g + QUAD] for k in range(3)] + [None] for w, g in places
        ]
        scores = attend_scores(units, blocks[...])
        if k + 1 < len(GROUPS):
            project(GROUPS[k + 1])
        weights = attend_weights(scores)
        for (w, g), mixed in zip(places, attend_values(units, weights, blocks[...])):
            attended[w * TOK : w * TOK + TOK, g : g + QUAD] = mixed
        here = slice(first * TOK, (first + count) * TOK)
        hidden = (held[here].astype(F32) + dot(attended[here], wout[...])).astype(BF16)
        for i, band in enumerate(group):
            part = hidden[i * size : i * size + size]
            at = early_place(band, 0) * TOK
            if band < 4:
                early[at : at + size] = part
            else:
                early[at : at + TOK] = part[0:TOK]
                late[(band - 4) * 256 : (band - 4) * 256 + 256] = part[TOK:]


def feed_forward(hidden, gain_mlp, gain_merge, wup, wdown, merged, place):
    hidden = hidden().astype(F32)
    normed = layer_norm(hidden, gain_mlp[...]).astype(BF16)
    yield
    total = hidden
    ahead = dot(normed, wup[:, 0:512])
    yield
    for n in range(0, MLP1, 512):
        inner = ahead
        if n + 512 < MLP1:
            ahead = dot(normed, wup[:, n + 512 : n + 1024])
        total = total + dot(gelu(inner).astype(BF16), wdown[n : n + 512, :])
        yield
    count = hidden.shape[0] // TOK
    refined = total.astype(BF16).astype(F32).reshape(count, 4, 16, C1)
    quads = jnp.concatenate([refined[:, i] for i in range(4)], axis=-1).reshape(count * 16, 4 * C1)
    merged[place * 16 : (place + count) * 16, :] = layer_norm(quads, gain_merge[...]).astype(BF16)
    yield


def rim_and_early(
    x_hbm, wqkv_hbm, wout_hbm, wup_hbm, wdown_hbm, wmerge_hbm,
    early, rim_rows, rim_cols, rim_corner, flag, gain_attn, gain_mlp, gain_merge, band_source, column_source, send_source,
    coarse, send_rows, send_cols, send_corner,
    xc, xr, wqkv, wout, wup, wdown, wmerge, blocks, qkv, attended, held, merged, sems,
):
    pairs = (
        (x_hbm.at[:, 32:48], xc), (x_hbm.at[ROWS - HALF : ROWS], xr), (wqkv_hbm, wqkv),
        (wup_hbm, wup), (wdown_hbm, wdown), (wout_hbm, wout), (wmerge_hbm, wmerge),
    )
    copies = [pltpu.make_async_copy(a, b, sems.at[i]) for i, (a, b) in enumerate(pairs)]
    for c in copies:
        c.start()
    blocks[...] = head_blocks()
    for c in copies[:4]:
        c.wait()

    def front():
        raw = jnp.concatenate([xr[...], rim_rows[...]], axis=0).reshape(BTOK, C1)
        rim = jnp.concatenate([rim_cols[240:256], rim_corner[...]], axis=0)
        tokens = [dot(picks(band_source[...], BTOK + 32), jnp.concatenate([raw, rim], axis=0))]
        perm = picks(column_source[...], 160)
        for b in range(BANDS - 1):
            raw = xc[b * WIN + HALF : b * WIN + HALF + WIN].reshape(128, C1)
            tokens.append(dot(perm, jnp.concatenate([raw, rim_cols[b * 32 + 16 : b * 32 + 48]], axis=0)))
        tokens = jnp.concatenate(tokens, axis=0)
        yield
        normed = layer_norm(tokens, gain_attn[...]).astype(BF16)
        yield
        for n in range(0, 3 * C1, 512):
            qkv[:, n : n + 512] = dot(normed, wqkv[:, n : n + 512]).astype(BF16)
            yield
        half_of = lambda axis: (lax.broadcasted_iota(jnp.int32, (TOK, QUAD), axis) >> 3) & 1
        bias = (half_of(0) != half_of(1)).astype(F32) * jnp.where(flag[0] == 1, -1e30, 0.0)
        for low, high in ((0, BWIN), (BWIN, 13)):
            places = [(w, g * QUAD) for w in range(low, high) for g in range(C1 // QUAD)]
            units = [
                [qkv[w * TOK : w * TOK + TOK, k * C1 + g : k * C1 + g + QUAD] for k in range(3)]
                + [bias if w < BWIN else None]
                for w, g in places
            ]
            scores = attend_scores(units, blocks[...])
            yield
            weights = attend_weights(scores)
            yield
            for (w, g), mixed in zip(places, attend_values(units, weights, blocks[...])):
                attended[w * TOK : w * TOK + TOK, g : g + QUAD] = mixed
            yield
        held[...] = (tokens + dot(attended[...], wout[...])).astype(BF16)
        yield

    def back():
        rest = (gain_mlp, gain_merge, wup, wdown, merged)
        yield from feed_forward(lambda: early[0 : 12 * TOK], *rest, 0)
        yield from feed_forward(lambda: early[12 * TOK : 23 * TOK], *rest, 12)

    for c in copies[4:6]:
        c.wait()
    drive(front(), back(), ORDER)
    for _ in feed_forward(lambda: held[...], gain_mlp, gain_merge, wup, wdown, merged, 23):
        pass
    copies[6].wait()
    for n in range(0, C2, 256):
        coarse[:, n : n + 256] = dot(merged[...], wmerge[:, n : n + 256]).astype(BF16)
    sent = dot(picks(send_source[...], EARLY * 16), coarse[...]).astype(BF16)
    send_rows[...] = sent[0:48]
    send_cols[...] = sent[48:112]
    send_corner[...] = sent[112:128]


def late_part(wup_hbm, wdown_hbm, wmerge_hbm, late, gain_mlp, gain_merge, coarse, wup, wdown, wmerge, merged, sems):
    pairs = ((wup_hbm, wup), (wdown_hbm, wdown), (wmerge_hbm, wmerge))
    copies = [pltpu.make_async_copy(a, b, sems.at[i]) for i, (a, b) in enumerate(pairs)]
    for c in copies:
        c.start()
    copies[0].wait()
    copies[1].wait()
    for _ in feed_forward(lambda: late[...], gain_mlp, gain_merge, wup, wdown, merged, 0):
        pass
    copies[2].wait()
    for n in range(0, C2, 256):
        coarse[:, n : n + 256] = dot(merged[...], wmerge[:, n : n + 256]).astype(BF16)


def section_two(
    wqkv_hbm, wout_hbm, early, late, rim_rows, rim_cols, rim_corner, flag, gain, source, send_source,
    result, send_rows, send_cols, send_corner,
    own, wqkv, wout, blocks, held, normed, qkv, attended, sems,
):
    groups = C2 // QUAD
    copies = []
    for g in range(groups):
        for k in range(3):
            here = slice(k * C2 + g * QUAD, k * C2 + g * QUAD + QUAD)
            copies.append(pltpu.make_async_copy(wqkv_hbm.at[:, here], wqkv.at[:, here], sems.at[g * 3 + k]))
    copies.append(pltpu.make_async_copy(wout_hbm, wout, sems.at[3 * groups]))
    for c in copies:
        c.start()
    blocks[...] = head_blocks()
    rim = jnp.concatenate([rim_rows[...], rim_cols[...], rim_corner[...]], axis=0)
    for band in range(BANDS):
        for col in range(BWIN):
            at = (band * BWIN + col) * 16
            if 4 <= band < BANDS - 1 and 1 <= col < INNER:
                place = ((band - 4) * 4 + col - 1) * 16
                own[at : at + 16] = late[place : place + 16]
            else:
                place = early_place(band, col) * 16
                own[at : at + 16] = early[place : place + 16]
    for i in range(CBANDS):
        here = slice(i * 192, i * 192 + 192)
        low, high = i * 192, min(i * 192 + 288, CTOK)
        tokens = dot(picks(source[here] - low, high - low), own[low:high]) + dot(picks(source[here] - CTOK, 128), rim)
        held[here] = tokens.astype(BF16)
        normed[here] = layer_norm(tokens, gain[...]).astype(BF16)
    half_of = lambda axis: (lax.broadcasted_iota(jnp.int32, (TOK, QUAD), axis) >> 5) & 1
    bias = (half_of(0) != half_of(1)).astype(F32) * jnp.where(flag[0] == 1, -1e30, 0.0)

    def project(g):
        for k in range(3):
            here = slice(k * C2 + g * QUAD, k * C2 + g * QUAD + QUAD)
            qkv[:, here] = dot(normed[...], wqkv[:, here]).astype(BF16)

    for c in copies[:3]:
        c.wait()
    project(0)
    for c in copies[3:]:
        c.wait()
    for g in range(groups):
        units = [
            [qkv[w * TOK : w * TOK + TOK, k * C2 + g * QUAD : k * C2 + g * QUAD + QUAD] for k in range(3)]
            + [bias if w >= CBWIN * (CBANDS - 1) else None]
            for w in range(CBWIN * CBANDS)
        ]
        scores = attend_scores(units, blocks[...])
        if g + 1 < groups:
            project(g + 1)
        weights = attend_weights(scores)
        for w, mixed in enumerate(attend_values(units, weights, blocks[...])):
            attended[w * TOK : w * TOK + TOK, g * QUAD : g * QUAD + QUAD] = mixed
    for n in range(0, C2, 256):
        here = slice(n, n + 256)
        result[:, here] = (held[:, here].astype(F32) + dot(attended[...], wout[:, here])).astype(BF16)
    sent = dot(picks(send_source[...], CTOK), result[...]).astype(BF16)
    send_rows[...] = sent[0:80]
    send_cols[...] = sent[80:192]
    send_corner[...] = sent[192:208]


def place(result, source, main):
    for i in range(CBANDS):
        here = slice(i * 192, i * 192 + 192)
        low = max(i - 1, 0) * 192
        main[here] = dot(picks(source[here] - low, here.stop - low), result[low : here.stop]).astype(BF16)


def join(main, rows, cols, corner, source, out):
    rim = jnp.concatenate([rows[...], cols[...], corner[...]], axis=0)
    out[...] = (main[...].astype(F32) + dot(picks(source[...], 208), rim)).astype(BF16)


HBM = pl.BlockSpec(memory_space=pltpu.HBM)
VM = pl.BlockSpec(memory_space=pltpu.VMEM)
SM = pl.BlockSpec(memory_space=pltpu.SMEM)


def whole(shape):
    return pl.BlockSpec(shape, lambda b: (0,) * len(shape))


def shift(values, axes, back):
    if isinstance(axes, str):
        count = lax.axis_size(axes)
        pairs = [(i, (i + 1) % count) for i in range(count)]
    else:
        lat, lon = (lax.axis_size(a) for a in axes)
        pairs = [(i * lon + j, ((i + 1) % lat) * lon + (j + 1) % lon) for i in range(lat) for j in range(lon)]
    if back:
        pairs = [(b, a) for a, b in pairs]
    return lax.ppermute(values, axes, pairs)


def sds(*shape):
    return jax.ShapeDtypeStruct(shape, BF16)


def cost(flops, weights):
    return pl.CostEstimate(flops=int(flops), bytes_accessed=int(weights), transcendentals=0)


def run_inner(tokens, w_qkv, w_out, gain):
    size = INNER * (BANDS - 1) * TOK
    return pl.pallas_call(
        attention_inner,
        grid=(1,),
        out_shape=[sds(23 * TOK, C1), sds(LATE * TOK, C1)],
        in_specs=[HBM] * 3 + [whole((1, C1)), whole((INNER * TOK, 1))],
        out_specs=[VM] * 2,
        scratch_shapes=[
            pltpu.VMEM((ROWS - HALF, COLS, C1), BF16),
            pltpu.VMEM((C1, 3 * C1), BF16),
            pltpu.VMEM((C1, C1), BF16),
            pltpu.VMEM((INNER * TOK, BTOK), BF16),
            pltpu.VMEM((QUAD, QUAD), BF16),
            pltpu.VMEM((size, 3 * C1), BF16),
            pltpu.VMEM((size, C1), BF16),
            pltpu.VMEM((size, C1), BF16),
            pltpu.SemaphoreType.DMA((6,)),
        ],
        cost_estimate=cost(12e9, 8e6),
        compiler_params=pltpu.CompilerParams(vmem_limit_bytes=VMEM_ONE << 20),
        name="attention_inner",
    )(tokens, w_qkv, w_out, gain.reshape(1, -1), jnp.asarray(inner_source()))


def run_rim(tokens, w_qkv, w_out, w_up, w_down, w_merge, early, rim_r, rim_c, rim_x, flag, gain_attn, gain_mlp, gain_merge):
    return pl.pallas_call(
        rim_and_early,
        grid=(1,),
        out_shape=[sds(EARLY * 16, C2), sds(48, C2), sds(64, C2), sds(16, C2)],
        in_specs=[HBM] * 6 + [VM] * 4
        + [SM] + [whole(n) for n in ((1, C1), (1, C1), (1, 4 * C1), (BTOK, 1), (TOK, 1), (128, 1))],
        out_specs=[VM] * 4,
        scratch_shapes=[
            pltpu.VMEM((ROWS, 16, C1), BF16),
            pltpu.VMEM((HALF, COLS, C1), BF16),
            pltpu.VMEM((C1, 3 * C1), BF16),
            pltpu.VMEM((C1, C1), BF16),
            pltpu.VMEM((C1, MLP1), BF16),
            pltpu.VMEM((MLP1, C1), BF16),
            pltpu.VMEM((4 * C1, C2), BF16),
            pltpu.VMEM((QUAD, QUAD), BF16),
            pltpu.VMEM((13 * TOK, 3 * C1), BF16),
            pltpu.VMEM((13 * TOK, C1), BF16),
            pltpu.VMEM((13 * TOK, C1), BF16),
            pltpu.VMEM((EARLY * 16, 4 * C1), BF16),
            pltpu.SemaphoreType.DMA((7,)),
        ],
        cost_estimate=cost(20e9, 14e6),
        compiler_params=pltpu.CompilerParams(vmem_limit_bytes=VMEM_ONE << 20),
        name="rim_and_early",
    )(
        tokens, w_qkv, w_out, w_up, w_down, w_merge, early, rim_r, rim_c, rim_x,
        flag, gain_attn.reshape(1, -1), gain_mlp.reshape(1, -1), gain_merge.reshape(1, -1),
        jnp.asarray(last_band_source()), jnp.asarray(last_column_source()), jnp.asarray(coarse_send_source()),
    )


def run_late(w_up, w_down, w_merge, late, gain_mlp, gain_merge):
    return pl.pallas_call(
        late_part,
        grid=(1,),
        out_shape=sds(LATE * 16, C2),
        in_specs=[HBM] * 3 + [VM, whole((1, C1)), whole((1, 4 * C1))],
        out_specs=VM,
        scratch_shapes=[
            pltpu.VMEM((C1, MLP1), BF16),
            pltpu.VMEM((MLP1, C1), BF16),
            pltpu.VMEM((4 * C1, C2), BF16),
            pltpu.VMEM((LATE * 16, 4 * C1), BF16),
            pltpu.SemaphoreType.DMA((3,)),
        ],
        cost_estimate=cost(5e9, 9e6),
        compiler_params=pltpu.CompilerParams(vmem_limit_bytes=VMEM_ONE << 20),
        name="late_part",
    )(w_up, w_down, w_merge, late, gain_mlp.reshape(1, -1), gain_merge.reshape(1, -1))


def run_two(w_qkv, w_out, early, late, rim_r, rim_c, rim_x, flag, gain):
    return pl.pallas_call(
        section_two,
        grid=(1,),
        out_shape=[sds(CTOK, C2), sds(80, C2), sds(112, C2), sds(16, C2)],
        in_specs=[HBM] * 2 + [VM] * 5 + [SM, whole((1, C2)), whole((CTOK, 1)), whole((208, 1))],
        out_specs=[VM] * 4,
        scratch_shapes=[
            pltpu.VMEM((CTOK, C2), BF16),
            pltpu.VMEM((C2, 3 * C2), BF16),
            pltpu.VMEM((C2, C2), BF16),
            pltpu.VMEM((QUAD, QUAD), BF16),
            pltpu.VMEM((CTOK, C2), BF16),
            pltpu.VMEM((CTOK, C2), BF16),
            pltpu.VMEM((CTOK, 3 * C2), BF16),
            pltpu.VMEM((CTOK, C2), BF16),
            pltpu.SemaphoreType.DMA((13,)),
        ],
        compiler_params=pltpu.CompilerParams(vmem_limit_bytes=VMEM_ONE << 20),
        name="section_two",
    )(
        w_qkv, w_out, early, late, rim_r, rim_c, rim_x, flag, gain.reshape(1, -1),
        jnp.asarray(coarse_source()), jnp.asarray(result_source()[CTOK:]),
    )


def run_place(result):
    return pl.pallas_call(
        place,
        grid=(1,),
        out_shape=sds(CTOK, C2),
        in_specs=[VM, whole((CTOK, 1))],
        out_specs=VM,
        cost_estimate=pl.CostEstimate(flops=2 * CTOK * 384 * C2, bytes_accessed=5 << 20, transcendentals=0),
        compiler_params=pltpu.CompilerParams(vmem_limit_bytes=32 << 20),
        name="place",
    )(result, jnp.asarray(result_source()[:CTOK]))


def run_join(main, rim_r, rim_c, rim_x):
    return pl.pallas_call(
        join,
        grid=(1,),
        out_shape=sds(CTOK, C2),
        in_specs=[VM, VM, VM, VM, whole((CTOK, 1))],
        out_specs=whole((CTOK, C2)),
        compiler_params=pltpu.CompilerParams(vmem_limit_bytes=32 << 20),
        name="join",
    )(main, rim_r, rim_c, rim_x, jnp.asarray(rim_source()))


def on_device(
    tokens, gain_attn1, w_qkv1, w_out1, gain_mlp1, w_up, w_down, gain_merge, w_merge, gain_attn2, w_qkv2, w_out2,
):
    flag = (lax.axis_index("lat") == lax.axis_size("lat") - 1).astype(jnp.int32).reshape(1)
    strip = lax.optimization_barrier(tokens[:, 0:HALF].reshape(256, C1))
    rim_c = shift(strip, "lon", True)
    rim_r = shift(tokens[0:HALF], "lat", True)
    rim_x = shift(strip[0:16], ("lat", "lon"), True)
    early, late = run_inner(tokens, w_qkv1, w_out1, gain_attn1)
    coarse, s_r, s_c, s_x = run_rim(
        tokens, w_qkv1, w_out1, w_up, w_down, w_merge, early, rim_r, rim_c, rim_x, flag, gain_attn1, gain_mlp1, gain_merge
    )
    coarse_late = run_late(w_up, w_down, w_merge, late, gain_mlp1, gain_merge)
    r_r = shift(s_r, "lat", True)
    r_c = shift(s_c, "lon", True)
    r_x = shift(s_x, ("lat", "lon"), True)
    result, s_r, s_c, s_x = run_two(w_qkv2, w_out2, coarse, coarse_late, r_r, r_c, r_x, flag, gain_attn2)
    r_r = shift(s_r, "lat", False)
    r_c = shift(s_c, "lon", False)
    r_x = shift(s_x, ("lat", "lon"), False)
    return run_join(run_place(result), r_r, r_c, r_x).reshape(CROWS, CCOLS, C2)


def solution(mesh):
    in_specs = (P("lat", "lon", None),) + (P(),) * 11
    return jax.shard_map(
        on_device, mesh=mesh, in_specs=in_specs, out_specs=P("lat", "lon", None), check_vma=False
    )
```

```python
import functools

import jax
import jax.numpy as jnp
import numpy as np
from jax import lax
from jax.experimental import pallas as pl
from jax.experimental.pallas import tpu as pltpu
from jax.sharding import PartitionSpec as P

HEAD_DIM = 64
WIN = 8
HALF = 4
TOK = WIN * WIN
NB = 2
QUAD = 4 * HEAD_DIM
ROWS, COLS, C1 = 64, 48, 512
MLP1 = 2048
C2 = 1024
CROWS, CCOLS = ROWS // 2, COLS // 2
BANDS, BWIN = ROWS // WIN, COLS // WIN
BTOK = WIN * COLS
CTOK = CROWS * CCOLS
STEPS = BANDS // NB
ORDER = "FBBFBFFFBFFBFFFBFBF"
CBANDS, CBWIN = CROWS // WIN, CCOLS // WIN
GRANT = 56
SCALE = HEAD_DIM**-0.5 * 1.4426950408889634
F32 = jnp.float32
BF16 = jnp.bfloat16


def band_source():
    out = np.zeros((BTOK, 1), np.int32)
    for o in range(BTOK):
        w, t = divmod(o, TOK)
        r = 2 * ((t >> 2) & 3) + ((t >> 4) & 1)
        c = WIN * w + 2 * (t & 3) + (t >> 5) + HALF
        out[o] = r * COLS + c if c < COLS else BTOK + r * HALF + c - COLS
    return out


def coarse_place(r, c):
    return ((r // 4) * BWIN + c // 4) * 16 + (r % 4) * 4 + c % 4


def coarse_send_source():
    out = np.full((128, 1), -1, np.int32)
    for i in range(2 * CCOLS):
        out[i] = coarse_place(i // CCOLS, i % CCOLS)
    for i in range(2 * CROWS):
        out[48 + i] = coarse_place(i // 2, i % 2)
    for i in range(4):
        out[112 + i] = coarse_place(i // 2, i % 2)
    return out


def coarse_source():
    out = np.zeros((CTOK, 1), np.int32)
    for o in range(CTOK):
        w, t = divmod(o, TOK)
        r = WIN * (w // CBWIN) + t // WIN + 2
        c = WIN * (w % CBWIN) + t % WIN + 2
        if r < CROWS and c < CCOLS:
            out[o] = coarse_place(r, c)
        elif c < CCOLS:
            out[o] = CTOK + (r - CROWS) * CCOLS + c
        elif r < CROWS:
            out[o] = CTOK + 48 + r * 2 + c - CCOLS
        else:
            out[o] = CTOK + 112 + (r - CROWS) * 2 + c - CCOLS
    return out


def window_place(r, c):
    return ((r // WIN) * CBWIN + c // WIN) * TOK + (r % WIN) * WIN + c % WIN


def result_source():
    out = np.full((976, 1), -1, np.int32)
    for r in range(HALF, CROWS):
        for c in range(HALF, CCOLS):
            out[r * CCOLS + c] = window_place(r - HALF, c - HALF)
    at = CTOK
    for r in range(CROWS - HALF, CROWS):
        for c in range(CCOLS - HALF):
            out[at] = window_place(r, c)
            at += 1
    for r in range(CROWS - HALF):
        for c in range(CCOLS - HALF, CCOLS):
            out[at] = window_place(r, c)
            at += 1
    for r in range(CROWS - HALF, CROWS):
        for c in range(CCOLS - HALF, CCOLS):
            out[at] = window_place(r, c)
            at += 1
    return out


def rim_source():
    out = np.full((CTOK, 1), -1, np.int32)
    for r in range(CROWS):
        for c in range(CCOLS):
            if r < HALF and c >= HALF:
                out[r * CCOLS + c] = r * (CCOLS - HALF) + c - HALF
            elif r >= HALF and c < HALF:
                out[r * CCOLS + c] = 80 + (r - HALF) * HALF + c
            elif r < HALF:
                out[r * CCOLS + c] = 192 + r * HALF + c
    return out


def picks(source, width):
    lanes = lax.broadcasted_iota(jnp.int32, (source.shape[0], width), 1)
    return (lanes == source).astype(F32).astype(BF16)


def layer_norm(values, scales):
    average = jnp.mean(values, axis=-1, keepdims=True)
    centred = values - average
    spread = jnp.mean(centred * centred, axis=-1, keepdims=True)
    return centred * lax.rsqrt(spread + 1e-05) * scales


def gelu(x):
    return 0.5 * x * (1.0 + jnp.tanh(x * (0.7978845608028654 + 0.035677408136300125 * (x * x))))


def dot(a, b):
    return jnp.dot(a, b, preferred_element_type=F32)


def head_blocks():
    rows = lax.broadcasted_iota(jnp.int32, (QUAD, QUAD), 0) // HEAD_DIM
    lanes = lax.broadcasted_iota(jnp.int32, (QUAD, QUAD), 1) // HEAD_DIM
    return (rows == lanes).astype(F32).astype(BF16)


def segment_max(scores):
    low = lax.broadcasted_iota(jnp.int32, (scores.shape[0], 128), 1) < HEAD_DIM
    out = []
    for t in range(0, QUAD, 128):
        part = scores[:, t : t + 128]
        first = jnp.max(jnp.where(low, part, -3e38), axis=1, keepdims=True)
        second = jnp.max(jnp.where(low, -3e38, part), axis=1, keepdims=True)
        out.append(jnp.where(low, first, second))
    return jnp.concatenate(out, axis=1)


def attend_scores(units, blocks):
    scores = []
    for queries, keys_in, _, bias in units:
        spread = jnp.concatenate([keys_in] * 4, axis=0) * blocks
        score = lax.dot_general(queries, spread, (((1,), (1,)), ((), ())), preferred_element_type=F32) * SCALE
        scores.append(score if bias is None else score + bias)
    return scores


def attend_weights(scores):
    return [jnp.exp2(score - segment_max(score)).astype(BF16) for score in scores]


def attend_values(units, weights, blocks):
    totals = dot(jnp.concatenate(weights, axis=0), blocks)
    mixed = []
    for i, (_, _, values_in, _) in enumerate(units):
        out = dot(weights[i], jnp.concatenate([values_in] * 4, axis=0) * blocks)
        mixed.append((out * (1.0 / totals[i * TOK : i * TOK + TOK])).astype(BF16))
    return mixed


def drive(first, second, order):
    streams = {"F": first, "B": second}
    for name in order:
        next(streams[name])
    for stream in (first, second):
        for _ in stream:
            pass


def section_one(
    x_hbm, wqkv_hbm, wout_hbm, wup_hbm, wdown_hbm, wmerge_hbm,
    rim_rows, rim_cols, rim_corner, flag, gain_attn, gain_mlp, gain_merge, source, send_source,
    coarse, send_rows, send_cols, send_corner,
    xs, hcs, wqkv, wout, wup, wdown, wmerge, perm, blocks, qkv, attended, held, merged, sems,
):
    step = pl.program_id(0)
    head = NB * WIN + HALF
    pairs = (
        (x_hbm.at[0:head], xs.at[0:head]), (wqkv_hbm, wqkv), (x_hbm.at[head:ROWS], xs.at[head:ROWS]),
        (wout_hbm, wout), (wup_hbm, wup), (wdown_hbm, wdown), (wmerge_hbm, wmerge),
    )
    copies = [pltpu.make_async_copy(a, b, sems.at[i]) for i, (a, b) in enumerate(pairs)]

    def front(opening):
        if opening:
            copies[0].wait()
        tokens = []
        for i in range(NB):
            top = (step * NB + i) * WIN + HALF
            raw = xs[pl.ds(top, WIN)].reshape(BTOK, C1)
            rim = hcs[pl.ds(pl.multiple_of((step * NB + i) * 32, 32), 32)]
            tokens.append(dot(perm[...], jnp.concatenate([raw, rim], axis=0)))
        tokens = jnp.concatenate(tokens, axis=0)
        yield
        normed = layer_norm(tokens, gain_attn[...]).astype(BF16)
        if opening:
            copies[1].wait()
        yield
        for n in range(0, 3 * C1, 512):
            qkv[:, n : n + 512] = dot(normed, wqkv[:, n : n + 512]).astype(BF16)
            yield
        half_of = lambda axis: (lax.broadcasted_iota(jnp.int32, (TOK, QUAD), axis) >> 3) & 1
        cut = jnp.where((flag[0] == 1) & (step == STEPS - 1), -1e30, 0.0)
        bias = (half_of(0) != half_of(1)).astype(F32) * cut
        for i in range(NB):
            places = [(i * BWIN + w, g * QUAD) for w in range(BWIN) for g in range(C1 // QUAD)]
            units = [
                [qkv[w * TOK : w * TOK + TOK, k * C1 + g : k * C1 + g + QUAD] for k in range(3)]
                + [bias if i == NB - 1 and not opening else None]
                for w, g in places
            ]
            scores = attend_scores(units, blocks[...])
            yield
            weights = attend_weights(scores)
            yield
            for (w, g), mixed in zip(places, attend_values(units, weights, blocks[...])):
                attended[w * TOK : w * TOK + TOK, g : g + QUAD] = mixed
            yield
        if opening:
            copies[3].wait()
        held[...] = (tokens + dot(attended[...], wout[...])).astype(BF16)
        if opening:
            for c in (2, 4, 5):
                copies[c].wait()
        yield

    def back():
        hidden = held[...].astype(F32)
        normed = layer_norm(hidden, gain_mlp[...]).astype(BF16)
        yield
        total = hidden
        ahead = dot(normed, wup[:, 0:512])
        yield
        for n in range(0, MLP1, 512):
            inner = ahead
            if n + 512 < MLP1:
                ahead = dot(normed, wup[:, n + 512 : n + 1024])
            total = total + dot(gelu(inner).astype(BF16), wdown[n : n + 512, :])
            yield
        refined = total.astype(BF16).astype(F32).reshape(NB * BWIN, 4, 16, C1)
        quads = jnp.concatenate([refined[:, i] for i in range(4)], axis=-1).reshape(NB * BTOK // 4, 4 * C1)
        rows = NB * BTOK // 4
        merged[pl.ds(pl.multiple_of((step - 1) * rows, rows), rows), :] = layer_norm(quads, gain_merge[...]).astype(BF16)
        yield

    @pl.when(step == 0)
    def _():
        for c in copies:
            c.start()
        perm[...] = picks(source[...], BTOK + 32)
        blocks[...] = head_blocks()
        xs[ROWS : ROWS + HALF] = rim_rows[...]
        hcs[0:240] = rim_cols[16:256]
        hcs[240:256] = rim_corner[...]
        drive(front(True), iter(()), "")

    @pl.when((step > 0) & (step < STEPS))
    def _():
        drive(front(False), back(), ORDER)

    @pl.when(step == STEPS)
    def _():
        drive(iter(()), back(), "")
        copies[6].wait()
        for n in range(0, C2, 256):
            coarse[:, n : n + 256] = dot(merged[...], wmerge[:, n : n + 256]).astype(BF16)
        sent = dot(picks(send_source[...], CTOK), coarse[...]).astype(BF16)
        send_rows[...] = sent[0:48]
        send_cols[...] = sent[48:112]
        send_corner[...] = sent[112:128]


def section_two(
    wqkv_hbm, wout_hbm, own, rim_rows, rim_cols, rim_corner, flag, gain, source, send_source,
    result, send_rows, send_cols, send_corner,
    wqkv, wout, blocks, held, normed, qkv, attended, sems,
):
    groups = C2 // QUAD
    copies = []
    for g in range(groups):
        for k in range(3):
            here = slice(k * C2 + g * QUAD, k * C2 + g * QUAD + QUAD)
            copies.append(pltpu.make_async_copy(wqkv_hbm.at[:, here], wqkv.at[:, here], sems.at[g * 3 + k]))
    copies.append(pltpu.make_async_copy(wout_hbm, wout, sems.at[3 * groups]))
    for c in copies:
        c.start()
    blocks[...] = head_blocks()
    rim = jnp.concatenate([rim_rows[...], rim_cols[...], rim_corner[...]], axis=0)
    for i in range(CBANDS):
        here = slice(i * 192, i * 192 + 192)
        low, high = i * 192, min(i * 192 + 288, CTOK)
        tokens = dot(picks(source[here] - low, high - low), own[low:high]) + dot(picks(source[here] - CTOK, 128), rim)
        held[here] = tokens.astype(BF16)
        normed[here] = layer_norm(tokens, gain[...]).astype(BF16)
    half_of = lambda axis: (lax.broadcasted_iota(jnp.int32, (TOK, QUAD), axis) >> 5) & 1
    bias = (half_of(0) != half_of(1)).astype(F32) * jnp.where(flag[0] == 1, -1e30, 0.0)

    def project(g):
        for k in range(3):
            here = slice(k * C2 + g * QUAD, k * C2 + g * QUAD + QUAD)
            qkv[:, here] = dot(normed[...], wqkv[:, here]).astype(BF16)

    for c in copies[:3]:
        c.wait()
    project(0)
    for c in copies[3:]:
        c.wait()
    for g in range(groups):
        units = [
            [qkv[w * TOK : w * TOK + TOK, k * C2 + g * QUAD : k * C2 + g * QUAD + QUAD] for k in range(3)]
            + [bias if w >= CBWIN * (CBANDS - 1) else None]
            for w in range(CBWIN * CBANDS)
        ]
        scores = attend_scores(units, blocks[...])
        if g + 1 < groups:
            project(g + 1)
        weights = attend_weights(scores)
        for w, mixed in enumerate(attend_values(units, weights, blocks[...])):
            attended[w * TOK : w * TOK + TOK, g * QUAD : g * QUAD + QUAD] = mixed
    for n in range(0, C2, 256):
        here = slice(n, n + 256)
        result[:, here] = (held[:, here].astype(F32) + dot(attended[...], wout[:, here])).astype(BF16)
    sent = dot(picks(send_source[...], CTOK), result[...]).astype(BF16)
    send_rows[...] = sent[0:80]
    send_cols[...] = sent[80:192]
    send_corner[...] = sent[192:208]


def place(result, source, main):
    for i in range(CBANDS):
        here = slice(i * 192, i * 192 + 192)
        low = max(i - 1, 0) * 192
        main[here] = dot(picks(source[here] - low, here.stop - low), result[low : here.stop]).astype(BF16)


def join(main, rows, cols, corner, source, out):
    rim = jnp.concatenate([rows[...], cols[...], corner[...]], axis=0)
    out[...] = (main[...].astype(F32) + dot(picks(source[...], 208), rim)).astype(BF16)


HBM = pl.BlockSpec(memory_space=pltpu.HBM)
VM = pl.BlockSpec(memory_space=pltpu.VMEM)
SM = pl.BlockSpec(memory_space=pltpu.SMEM)


def whole(shape):
    return pl.BlockSpec(shape, lambda b: (0,) * len(shape))


def shift(values, axes, back):
    if isinstance(axes, str):
        count = lax.axis_size(axes)
        pairs = [(i, (i + 1) % count) for i in range(count)]
    else:
        lat, lon = (lax.axis_size(a) for a in axes)
        pairs = [(i * lon + j, ((i + 1) % lat) * lon + (j + 1) % lon) for i in range(lat) for j in range(lon)]
    if back:
        pairs = [(b, a) for a, b in pairs]
    return lax.ppermute(values, axes, pairs)


def sds(*shape):
    return jax.ShapeDtypeStruct(shape, BF16)


def run_one(tokens, w_qkv, w_out, w_up, w_down, w_merge, rim_r, rim_c, rim_x, flag, gain_attn, gain_mlp, gain_merge):
    return pl.pallas_call(
        section_one,
        grid=(STEPS + 1,),
        out_shape=[sds(CTOK, C2), sds(48, C2), sds(64, C2), sds(16, C2)],
        in_specs=[HBM] * 6 + [VM] * 3
        + [SM, whole((1, C1)), whole((1, C1)), whole((1, 4 * C1)), whole((BTOK, 1)), whole((128, 1))],
        out_specs=[VM] * 4,
        scratch_shapes=[
            pltpu.VMEM((ROWS + HALF, COLS, C1), BF16),
            pltpu.VMEM((256, C1), BF16),
            pltpu.VMEM((C1, 3 * C1), BF16),
            pltpu.VMEM((C1, C1), BF16),
            pltpu.VMEM((C1, MLP1), BF16),
            pltpu.VMEM((MLP1, C1), BF16),
            pltpu.VMEM((4 * C1, C2), BF16),
            pltpu.VMEM((BTOK, BTOK + 32), BF16),
            pltpu.VMEM((QUAD, QUAD), BF16),
            pltpu.VMEM((NB * BTOK, 3 * C1), BF16),
            pltpu.VMEM((NB * BTOK, C1), BF16),
            pltpu.VMEM((NB * BTOK, C1), BF16),
            pltpu.VMEM((CTOK, 4 * C1), BF16),
            pltpu.SemaphoreType.DMA((7,)),
        ],
        compiler_params=pltpu.CompilerParams(vmem_limit_bytes=GRANT << 20),
        name="section_one",
    )(
        tokens, w_qkv, w_out, w_up, w_down, w_merge, rim_r, rim_c, rim_x,
        flag, gain_attn.reshape(1, -1), gain_mlp.reshape(1, -1), gain_merge.reshape(1, -1),
        jnp.asarray(band_source()), jnp.asarray(coarse_send_source()),
    )


def run_two(w_qkv, w_out, coarse, rim_r, rim_c, rim_x, flag, gain):
    return pl.pallas_call(
        section_two,
        grid=(1,),
        out_shape=[sds(CTOK, C2), sds(80, C2), sds(112, C2), sds(16, C2)],
        in_specs=[HBM] * 2 + [VM] * 4 + [SM, whole((1, C2)), whole((CTOK, 1)), whole((208, 1))],
        out_specs=[VM] * 4,
        scratch_shapes=[
            pltpu.VMEM((C2, 3 * C2), BF16),
            pltpu.VMEM((C2, C2), BF16),
            pltpu.VMEM((QUAD, QUAD), BF16),
            pltpu.VMEM((CTOK, C2), BF16),
            pltpu.VMEM((CTOK, C2), BF16),
            pltpu.VMEM((CTOK, 3 * C2), BF16),
            pltpu.VMEM((CTOK, C2), BF16),
            pltpu.SemaphoreType.DMA((13,)),
        ],
        compiler_params=pltpu.CompilerParams(vmem_limit_bytes=48 << 20),
        name="section_two",
    )(
        w_qkv, w_out, coarse, rim_r, rim_c, rim_x, flag, gain.reshape(1, -1),
        jnp.asarray(coarse_source()), jnp.asarray(result_source()[CTOK:]),
    )


def run_place(result):
    return pl.pallas_call(
        place,
        grid=(1,),
        out_shape=sds(CTOK, C2),
        in_specs=[VM, whole((CTOK, 1))],
        out_specs=VM,
        cost_estimate=pl.CostEstimate(flops=2 * CTOK * 384 * C2, bytes_accessed=5 << 20, transcendentals=0),
        compiler_params=pltpu.CompilerParams(vmem_limit_bytes=32 << 20),
        name="place",
    )(result, jnp.asarray(result_source()[:CTOK]))


def run_join(main, rim_r, rim_c, rim_x):
    return pl.pallas_call(
        join,
        grid=(1,),
        out_shape=sds(CTOK, C2),
        in_specs=[VM, VM, VM, VM, whole((CTOK, 1))],
        out_specs=whole((CTOK, C2)),
        compiler_params=pltpu.CompilerParams(vmem_limit_bytes=32 << 20),
        name="join",
    )(main, rim_r, rim_c, rim_x, jnp.asarray(rim_source()))


def on_device(
    tokens, gain_attn1, w_qkv1, w_out1, gain_mlp1, w_up, w_down, gain_merge, w_merge, gain_attn2, w_qkv2, w_out2,
):
    flag = (lax.axis_index("lat") == lax.axis_size("lat") - 1).astype(jnp.int32).reshape(1)
    strip = lax.optimization_barrier(tokens[:, 0:HALF].reshape(256, C1))
    rim_c = shift(strip, "lon", True)
    rim_r = shift(tokens[0:HALF], "lat", True)
    rim_x = shift(strip[0:16], ("lat", "lon"), True)
    coarse, s_r, s_c, s_x = run_one(
        tokens, w_qkv1, w_out1, w_up, w_down, w_merge, rim_r, rim_c, rim_x, flag, gain_attn1, gain_mlp1, gain_merge
    )
    r_r = shift(s_r, "lat", True)
    r_c = shift(s_c, "lon", True)
    r_x = shift(s_x, ("lat", "lon"), True)
    result, s_r, s_c, s_x = run_two(w_qkv2, w_out2, coarse, r_r, r_c, r_x, flag, gain_attn2)
    r_r = shift(s_r, "lat", False)
    r_c = shift(s_c, "lon", False)
    r_x = shift(s_x, ("lat", "lon"), False)
    return run_join(run_place(result), r_r, r_c, r_x).reshape(CROWS, CCOLS, C2)


def solution(mesh):
    in_specs = (P("lat", "lon", None),) + (P(),) * 11
    return jax.shard_map(
        on_device, mesh=mesh, in_specs=in_specs, out_specs=P("lat", "lon", None), check_vma=False
    )
```

```python
import functools

import jax
import jax.numpy as jnp
import numpy as np
from jax import lax
from jax.experimental import pallas as pl
from jax.experimental.pallas import tpu as pltpu
from jax.sharding import PartitionSpec as P

HEAD_DIM = 64
WIN = 8
HALF = 4
TOK = WIN * WIN
NB = 2
QUAD = 4 * HEAD_DIM
ROWS, COLS, C1 = 64, 48, 512
MLP1 = 2048
C2 = 1024
CROWS, CCOLS = ROWS // 2, COLS // 2
BANDS, BWIN = ROWS // WIN, COLS // WIN
BTOK = WIN * COLS
CTOK = CROWS * CCOLS
STEPS = BANDS // NB
ORDER = "FBBFBFFFBFFBFFFBFBF"
CBANDS, CBWIN = CROWS // WIN, CCOLS // WIN
GRANT = 50
SCALE = HEAD_DIM**-0.5 * 1.4426950408889634
F32 = jnp.float32
BF16 = jnp.bfloat16


def coarse_place(r, c):
    return ((r // 4) * BWIN + c // 4) * 16 + (r % 4) * 4 + c % 4


def coarse_source():
    out = np.zeros((CTOK, 1), np.int32)
    for o in range(CTOK):
        w, t = divmod(o, TOK)
        r = WIN * (w // CBWIN) + t // WIN + 2
        c = WIN * (w % CBWIN) + t % WIN + 2
        if r < CROWS and c < CCOLS:
            out[o] = coarse_place(r, c)
        elif c < CCOLS:
            out[o] = CTOK + (r - CROWS) * CCOLS + c
        elif r < CROWS:
            out[o] = CTOK + 48 + r * 2 + c - CCOLS
        else:
            out[o] = CTOK + 112 + (r - CROWS) * 2 + c - CCOLS
    return out


def window_place(r, c):
    return ((r // WIN) * CBWIN + c // WIN) * TOK + (r % WIN) * WIN + c % WIN


def result_source():
    out = np.full((976, 1), -1, np.int32)
    for r in range(HALF, CROWS):
        for c in range(HALF, CCOLS):
            out[r * CCOLS + c] = window_place(r - HALF, c - HALF)
    at = CTOK
    for r in range(CROWS - HALF, CROWS):
        for c in range(CCOLS - HALF):
            out[at] = window_place(r, c)
            at += 1
    for r in range(CROWS - HALF):
        for c in range(CCOLS - HALF, CCOLS):
            out[at] = window_place(r, c)
            at += 1
    for r in range(CROWS - HALF, CROWS):
        for c in range(CCOLS - HALF, CCOLS):
            out[at] = window_place(r, c)
            at += 1
    return out


def rim_source():
    out = np.full((CTOK, 1), -1, np.int32)
    for r in range(CROWS):
        for c in range(CCOLS):
            if r < HALF and c >= HALF:
                out[r * CCOLS + c] = r * (CCOLS - HALF) + c - HALF
            elif r >= HALF and c < HALF:
                out[r * CCOLS + c] = 80 + (r - HALF) * HALF + c
            elif r < HALF:
                out[r * CCOLS + c] = 192 + r * HALF + c
    return out


def band_source():
    o = lax.broadcasted_iota(jnp.int32, (BTOK, 1), 0)
    t = o & (TOK - 1)
    r = 2 * ((t >> 2) & 3) + ((t >> 4) & 1)
    c = (o >> 6) * WIN + 2 * (t & 3) + (t >> 5) + HALF
    return jnp.where(c < COLS, r * COLS + c, BTOK + r * HALF + c - COLS)


def coarse_send_source():
    i = lax.broadcasted_iota(jnp.int32, (128, 1), 0)
    second = (i >= CCOLS).astype(jnp.int32)
    place = lambda r, c: ((r >> 2) * BWIN + (c >> 2)) * 16 + (r & 3) * 4 + (c & 3)
    rows = place(second, i - CCOLS * second)
    cols = place((i - 48) >> 1, i & 1)
    corner = jnp.where(i < 116, place((i - 112) >> 1, i & 1), -1)
    return jnp.where(i < 48, rows, jnp.where(i < 112, cols, corner))


def picks(source, width):
    lanes = lax.broadcasted_iota(jnp.int32, (source.shape[0], width), 1)
    return (lanes == source).astype(F32).astype(BF16)


def layer_norm(values, scales):
    average = jnp.mean(values, axis=-1, keepdims=True)
    centred = values - average
    spread = jnp.mean(centred * centred, axis=-1, keepdims=True)
    return centred * lax.rsqrt(spread + 1e-05) * scales


def gelu(x):
    return 0.5 * x * (1.0 + jnp.tanh(x * (0.7978845608028654 + 0.035677408136300125 * (x * x))))


def dot(a, b):
    return jnp.dot(a, b, preferred_element_type=F32)


def head_blocks():
    rows = lax.broadcasted_iota(jnp.int32, (QUAD, QUAD), 0) // HEAD_DIM
    lanes = lax.broadcasted_iota(jnp.int32, (QUAD, QUAD), 1) // HEAD_DIM
    return (rows == lanes).astype(F32).astype(BF16)


def segment_max(scores):
    low = lax.broadcasted_iota(jnp.int32, (scores.shape[0], 128), 1) < HEAD_DIM
    out = []
    for t in range(0, QUAD, 128):
        part = scores[:, t : t + 128]
        first = jnp.max(jnp.where(low, part, -3e38), axis=1, keepdims=True)
        second = jnp.max(jnp.where(low, -3e38, part), axis=1, keepdims=True)
        out.append(jnp.where(low, first, second))
    return jnp.concatenate(out, axis=1)


def attend_scores(units, blocks):
    scores = []
    for queries, keys_in, _, bias in units:
        spread = jnp.concatenate([keys_in] * 4, axis=0) * blocks
        score = lax.dot_general(queries, spread, (((1,), (1,)), ((), ())), preferred_element_type=F32) * SCALE
        scores.append(score if bias is None else score + bias)
    return scores


def attend_weights(scores):
    return [jnp.exp2(score - segment_max(score)).astype(BF16) for score in scores]


def attend_values(units, weights, blocks):
    totals = dot(jnp.concatenate(weights, axis=0), blocks)
    mixed = []
    for i, (_, _, values_in, _) in enumerate(units):
        out = dot(weights[i], jnp.concatenate([values_in] * 4, axis=0) * blocks)
        mixed.append((out * (1.0 / totals[i * TOK : i * TOK + TOK])).astype(BF16))
    return mixed


def drive(first, second, order):
    streams = {"F": first, "B": second}
    for name in order:
        next(streams[name])
    for stream in (first, second):
        for _ in stream:
            pass


def section_one(
    x_hbm, wqkv_hbm, wout_hbm, wup_hbm, wdown_hbm, wmerge_hbm,
    rim_rows, rim_cols, rim_corner, flag, gains,
    coarse, send_rows, send_cols, send_corner,
    xs, hcs, wqkv, wout, wup, wdown, wmerge, perm, blocks, qkv, attended, held, merged, sems,
):
    step = pl.program_id(0)
    head = NB * WIN + HALF
    pairs = (
        (x_hbm.at[0:head], xs.at[0:head]), (wqkv_hbm, wqkv), (x_hbm.at[head:ROWS], xs.at[head:ROWS]),
        (wout_hbm, wout), (wup_hbm, wup), (wdown_hbm, wdown), (wmerge_hbm, wmerge),
    )
    copies = [pltpu.make_async_copy(a, b, sems.at[i]) for i, (a, b) in enumerate(pairs)]

    def front(opening):
        if opening:
            copies[0].wait()
        tokens = []
        for i in range(NB):
            top = (step * NB + i) * WIN + HALF
            raw = xs[pl.ds(top, WIN)].reshape(BTOK, C1)
            rim = hcs[pl.ds(pl.multiple_of((step * NB + i) * 32, 32), 32)]
            tokens.append(dot(perm[...], jnp.concatenate([raw, rim], axis=0)))
        tokens = jnp.concatenate(tokens, axis=0)
        yield
        normed = layer_norm(tokens, gains[:, 0:C1]).astype(BF16)
        if opening:
            copies[1].wait()
        yield
        for n in range(0, 3 * C1, 512):
            qkv[:, n : n + 512] = dot(normed, wqkv[:, n : n + 512]).astype(BF16)
            yield
        half_of = lambda axis: (lax.broadcasted_iota(jnp.int32, (TOK, QUAD), axis) >> 3) & 1
        cut = jnp.where((flag[0] == 1) & (step == STEPS - 1), -1e30, 0.0)
        bias = (half_of(0) != half_of(1)).astype(F32) * cut
        for i in range(NB):
            places = [(i * BWIN + w, g * QUAD) for w in range(BWIN) for g in range(C1 // QUAD)]
            units = [
                [qkv[w * TOK : w * TOK + TOK, k * C1 + g : k * C1 + g + QUAD] for k in range(3)]
                + [bias if i == NB - 1 and not opening else None]
                for w, g in places
            ]
            scores = attend_scores(units, blocks[...])
            yield
            weights = attend_weights(scores)
            yield
            for (w, g), mixed in zip(places, attend_values(units, weights, blocks[...])):
                attended[w * TOK : w * TOK + TOK, g : g + QUAD] = mixed
            yield
        if opening:
            copies[3].wait()
        held[...] = (tokens + dot(attended[...], wout[...])).astype(BF16)
        if opening:
            for c in (2, 4, 5):
                copies[c].wait()
        yield

    def back():
        hidden = held[...].astype(F32)
        normed = layer_norm(hidden, gains[:, C1 : 2 * C1]).astype(BF16)
        yield
        total = hidden
        ahead = dot(normed, wup[:, 0:512])
        yield
        for n in range(0, MLP1, 512):
            inner = ahead
            if n + 512 < MLP1:
                ahead = dot(normed, wup[:, n + 512 : n + 1024])
            total = total + dot(gelu(inner).astype(BF16), wdown[n : n + 512, :])
            yield
        refined = total.astype(BF16).astype(F32).reshape(NB * BWIN, 4, 16, C1)
        quads = jnp.concatenate([refined[:, i] for i in range(4)], axis=-1).reshape(NB * BTOK // 4, 4 * C1)
        rows = NB * BTOK // 4
        merged[pl.ds(pl.multiple_of((step - 1) * rows, rows), rows), :] = layer_norm(quads, gains[:, 2 * C1 :]).astype(BF16)
        yield

    @pl.when(step == 0)
    def _():
        for c in copies:
            c.start()
        perm[...] = picks(band_source(), BTOK + 32)
        blocks[...] = head_blocks()
        xs[ROWS : ROWS + HALF] = rim_rows[...]
        hcs[0:240] = rim_cols[16:256]
        hcs[240:256] = rim_corner[...]
        drive(front(True), iter(()), "")

    @pl.when((step > 0) & (step < STEPS))
    def _():
        drive(front(False), back(), ORDER)

    @pl.when(step == STEPS)
    def _():
        drive(iter(()), back(), "")
        copies[6].wait()
        for n in range(0, C2, 256):
            coarse[:, n : n + 256] = dot(merged[...], wmerge[:, n : n + 256]).astype(BF16)
        sent = dot(picks(coarse_send_source(), CTOK), coarse[...]).astype(BF16)
        send_rows[...] = sent[0:48]
        send_cols[...] = sent[48:112]
        send_corner[...] = sent[112:128]


def section_two(
    wqkv_hbm, wout_hbm, own, rim_rows, rim_cols, rim_corner, flag, gain, source, send_source,
    result, send_rows, send_cols, send_corner,
    wqkv, wout, blocks, held, normed, qkv, attended, sems,
):
    groups = C2 // QUAD
    copies = []
    for g in range(groups):
        for k in range(3):
            here = slice(k * C2 + g * QUAD, k * C2 + g * QUAD + QUAD)
            copies.append(pltpu.make_async_copy(wqkv_hbm.at[:, here], wqkv.at[:, here], sems.at[g * 3 + k]))
    copies.append(pltpu.make_async_copy(wout_hbm, wout, sems.at[3 * groups]))
    for c in copies:
        c.start()
    blocks[...] = head_blocks()
    rim = jnp.concatenate([rim_rows[...], rim_cols[...], rim_corner[...]], axis=0)
    for i in range(CBANDS):
        here = slice(i * 192, i * 192 + 192)
        low, high = i * 192, min(i * 192 + 288, CTOK)
        tokens = dot(picks(source[here] - low, high - low), own[low:high]) + dot(picks(source[here] - CTOK, 128), rim)
        held[here] = tokens.astype(BF16)
        normed[here] = layer_norm(tokens, gain[...]).astype(BF16)
    half_of = lambda axis: (lax.broadcasted_iota(jnp.int32, (TOK, QUAD), axis) >> 5) & 1
    bias = (half_of(0) != half_of(1)).astype(F32) * jnp.where(flag[0] == 1, -1e30, 0.0)

    def project(g):
        for k in range(3):
            here = slice(k * C2 + g * QUAD, k * C2 + g * QUAD + QUAD)
            qkv[:, here] = dot(normed[...], wqkv[:, here]).astype(BF16)

    for c in copies[:3]:
        c.wait()
    project(0)
    for c in copies[3:]:
        c.wait()
    for g in range(groups):
        units = [
            [qkv[w * TOK : w * TOK + TOK, k * C2 + g * QUAD : k * C2 + g * QUAD + QUAD] for k in range(3)]
            + [bias if w >= CBWIN * (CBANDS - 1) else None]
            for w in range(CBWIN * CBANDS)
        ]
        scores = attend_scores(units, blocks[...])
        if g + 1 < groups:
            project(g + 1)
        weights = attend_weights(scores)
        for w, mixed in enumerate(attend_values(units, weights, blocks[...])):
            attended[w * TOK : w * TOK + TOK, g * QUAD : g * QUAD + QUAD] = mixed
    for n in range(0, C2, 256):
        here = slice(n, n + 256)
        result[:, here] = (held[:, here].astype(F32) + dot(attended[...], wout[:, here])).astype(BF16)
    sent = dot(picks(send_source[...], CTOK), result[...]).astype(BF16)
    send_rows[...] = sent[0:80]
    send_cols[...] = sent[80:192]
    send_corner[...] = sent[192:208]


def place(result, source, main):
    for i in range(CBANDS):
        here = slice(i * 192, i * 192 + 192)
        low = max(i - 1, 0) * 192
        main[here] = dot(picks(source[here] - low, here.stop - low), result[low : here.stop]).astype(BF16)


def join(main, rows, cols, corner, source, out):
    rim = jnp.concatenate([rows[...], cols[...], corner[...]], axis=0)
    out[...] = (main[...].astype(F32) + dot(picks(source[...], 208), rim)).astype(BF16)


HBM = pl.BlockSpec(memory_space=pltpu.HBM)
VM = pl.BlockSpec(memory_space=pltpu.VMEM)
SM = pl.BlockSpec(memory_space=pltpu.SMEM)


def whole(shape):
    return pl.BlockSpec(shape, lambda b: (0,) * len(shape))


def shift(values, axes, back):
    if isinstance(axes, str):
        count = lax.axis_size(axes)
        pairs = [(i, (i + 1) % count) for i in range(count)]
    else:
        lat, lon = (lax.axis_size(a) for a in axes)
        pairs = [(i * lon + j, ((i + 1) % lat) * lon + (j + 1) % lon) for i in range(lat) for j in range(lon)]
    if back:
        pairs = [(b, a) for a, b in pairs]
    return lax.ppermute(values, axes, pairs)


def sds(*shape):
    return jax.ShapeDtypeStruct(shape, BF16)


def run_one(tokens, w_qkv, w_out, w_up, w_down, w_merge, rim_r, rim_c, rim_x, flag, gains):
    return pl.pallas_call(
        section_one,
        grid=(STEPS + 1,),
        out_shape=[sds(CTOK, C2), sds(48, C2), sds(64, C2), sds(16, C2)],
        in_specs=[HBM] * 6 + [VM] * 3
        + [SM, whole((1, 6 * C1))],
        out_specs=[VM] * 4,
        scratch_shapes=[
            pltpu.VMEM((ROWS + HALF, COLS, C1), BF16),
            pltpu.VMEM((256, C1), BF16),
            pltpu.VMEM((C1, 3 * C1), BF16),
            pltpu.VMEM((C1, C1), BF16),
            pltpu.VMEM((C1, MLP1), BF16),
            pltpu.VMEM((MLP1, C1), BF16),
            pltpu.VMEM((4 * C1, C2), BF16),
            pltpu.VMEM((BTOK, BTOK + 32), BF16),
            pltpu.VMEM((QUAD, QUAD), BF16),
            pltpu.VMEM((NB * BTOK, 3 * C1), BF16),
            pltpu.VMEM((NB * BTOK, C1), BF16),
            pltpu.VMEM((NB * BTOK, C1), BF16),
            pltpu.VMEM((CTOK, 4 * C1), BF16),
            pltpu.SemaphoreType.DMA((7,)),
        ],
        compiler_params=pltpu.CompilerParams(vmem_limit_bytes=GRANT << 20),
        name="section_one",
    )(
        tokens, w_qkv, w_out, w_up, w_down, w_merge, rim_r, rim_c, rim_x,
        flag, gains,
    )


def run_two(w_qkv, w_out, coarse, rim_r, rim_c, rim_x, flag, gain):
    return pl.pallas_call(
        section_two,
        grid=(1,),
        out_shape=[sds(CTOK, C2), sds(80, C2), sds(112, C2), sds(16, C2)],
        in_specs=[HBM] * 2 + [VM] * 4 + [SM, whole((1, C2)), whole((CTOK, 1)), whole((208, 1))],
        out_specs=[VM] * 4,
        scratch_shapes=[
            pltpu.VMEM((C2, 3 * C2), BF16),
            pltpu.VMEM((C2, C2), BF16),
            pltpu.VMEM((QUAD, QUAD), BF16),
            pltpu.VMEM((CTOK, C2), BF16),
            pltpu.VMEM((CTOK, C2), BF16),
            pltpu.VMEM((CTOK, 3 * C2), BF16),
            pltpu.VMEM((CTOK, C2), BF16),
            pltpu.SemaphoreType.DMA((13,)),
        ],
        compiler_params=pltpu.CompilerParams(vmem_limit_bytes=48 << 20),
        name="section_two",
    )(
        w_qkv, w_out, coarse, rim_r, rim_c, rim_x, flag, gain.reshape(1, -1),
        jnp.asarray(coarse_source()), jnp.asarray(result_source()[CTOK:]),
    )


def run_place(result):
    return pl.pallas_call(
        place,
        grid=(1,),
        out_shape=sds(CTOK, C2),
        in_specs=[VM, whole((CTOK, 1))],
        out_specs=VM,
        cost_estimate=pl.CostEstimate(flops=2 * CTOK * 384 * C2, bytes_accessed=5 << 20, transcendentals=0),
        compiler_params=pltpu.CompilerParams(vmem_limit_bytes=32 << 20),
        name="place",
    )(result, jnp.asarray(result_source()[:CTOK]))


def run_join(main, rim_r, rim_c, rim_x):
    return pl.pallas_call(
        join,
        grid=(1,),
        out_shape=sds(CTOK, C2),
        in_specs=[VM, VM, VM, VM, whole((CTOK, 1))],
        out_specs=whole((CTOK, C2)),
        compiler_params=pltpu.CompilerParams(vmem_limit_bytes=32 << 20),
        name="join",
    )(main, rim_r, rim_c, rim_x, jnp.asarray(rim_source()))


def on_device(
    tokens, gain_attn1, w_qkv1, w_out1, gain_mlp1, w_up, w_down, gain_merge, w_merge, gain_attn2, w_qkv2, w_out2,
):
    flag = (lax.axis_index("lat") == lax.axis_size("lat") - 1).astype(jnp.int32).reshape(1)
    strip = lax.optimization_barrier(tokens[:, 0:HALF].reshape(256, C1))
    rim_c = shift(strip, "lon", True)
    rim_r = shift(tokens[0:HALF], "lat", True)
    rim_x = shift(strip[0:16], ("lat", "lon"), True)
    coarse, s_r, s_c, s_x = run_one(
        tokens, w_qkv1, w_out1, w_up, w_down, w_merge, rim_r, rim_c, rim_x, flag,
        jnp.concatenate([gain_attn1, gain_mlp1, gain_merge]).reshape(1, -1),
    )
    r_r = shift(s_r, "lat", True)
    r_c = shift(s_c, "lon", True)
    r_x = shift(s_x, ("lat", "lon"), True)
    result, s_r, s_c, s_x = run_two(w_qkv2, w_out2, coarse, r_r, r_c, r_x, flag, gain_attn2)
    r_r = shift(s_r, "lat", False)
    r_c = shift(s_c, "lon", False)
    r_x = shift(s_x, ("lat", "lon"), False)
    return run_join(run_place(result), r_r, r_c, r_x).reshape(CROWS, CCOLS, C2)


def solution(mesh):
    in_specs = (P("lat", "lon", None),) + (P(),) * 11
    return jax.shard_map(
        on_device, mesh=mesh, in_specs=in_specs, out_specs=P("lat", "lon", None), check_vma=False
    )
```

```python
import functools

import jax
import jax.numpy as jnp
import numpy as np
from jax import lax
from jax.experimental import pallas as pl
from jax.experimental.pallas import tpu as pltpu
from jax.sharding import PartitionSpec as P

HEAD_DIM = 64
WIN = 8
HALF = 4
TOK = WIN * WIN
NB = 2
QUAD = 4 * HEAD_DIM
ROWS, COLS, C1 = 64, 48, 512
MLP1 = 2048
C2 = 1024
CROWS, CCOLS = ROWS // 2, COLS // 2
BANDS, BWIN = ROWS // WIN, COLS // WIN
BTOK = WIN * COLS
CTOK = CROWS * CCOLS
STEPS = BANDS // NB
ORDER = "FBBFBFFFBFFBFFFBFBF"
CBANDS, CBWIN = CROWS // WIN, CCOLS // WIN
GRANT = 50
SCALE = HEAD_DIM**-0.5 * 1.4426950408889634
F32 = jnp.float32
BF16 = jnp.bfloat16


def coarse_place(r, c):
    return ((r // 4) * BWIN + c // 4) * 16 + (r % 4) * 4 + c % 4


def coarse_source():
    out = np.zeros((CTOK, 1), np.int32)
    for o in range(CTOK):
        w, t = divmod(o, TOK)
        r = WIN * (w // CBWIN) + t // WIN + 2
        c = WIN * (w % CBWIN) + t % WIN + 2
        if r < CROWS and c < CCOLS:
            out[o] = coarse_place(r, c)
        elif c < CCOLS:
            out[o] = CTOK + (r - CROWS) * CCOLS + c
        elif r < CROWS:
            out[o] = CTOK + 48 + r * 2 + c - CCOLS
        else:
            out[o] = CTOK + 112 + (r - CROWS) * 2 + c - CCOLS
    return out


def window_place(r, c):
    return ((r // WIN) * CBWIN + c // WIN) * TOK + (r % WIN) * WIN + c % WIN


def result_source():
    out = np.full((976, 1), -1, np.int32)
    for r in range(HALF, CROWS):
        for c in range(HALF, CCOLS):
            out[r * CCOLS + c] = window_place(r - HALF, c - HALF)
    at = CTOK
    for r in range(CROWS - HALF, CROWS):
        for c in range(CCOLS - HALF):
            out[at] = window_place(r, c)
            at += 1
    for r in range(CROWS - HALF):
        for c in range(CCOLS - HALF, CCOLS):
            out[at] = window_place(r, c)
            at += 1
    for r in range(CROWS - HALF, CROWS):
        for c in range(CCOLS - HALF, CCOLS):
            out[at] = window_place(r, c)
            at += 1
    return out


def rim_source():
    out = np.full((CTOK, 1), -1, np.int32)
    for r in range(CROWS):
        for c in range(CCOLS):
            if r < HALF and c >= HALF:
                out[r * CCOLS + c] = r * (CCOLS - HALF) + c - HALF
            elif r >= HALF and c < HALF:
                out[r * CCOLS + c] = 80 + (r - HALF) * HALF + c
            elif r < HALF:
                out[r * CCOLS + c] = 192 + r * HALF + c
    return out


def band_source():
    o = lax.broadcasted_iota(jnp.int32, (BTOK, 1), 0)
    t = o & (TOK - 1)
    r = 2 * ((t >> 2) & 3) + ((t >> 4) & 1)
    c = (o >> 6) * WIN + 2 * (t & 3) + (t >> 5) + HALF
    return jnp.where(c < COLS, r * COLS + c, BTOK + r * HALF + c - COLS)


def coarse_send_source():
    i = lax.broadcasted_iota(jnp.int32, (128, 1), 0)
    second = (i >= CCOLS).astype(jnp.int32)
    place = lambda r, c: ((r >> 2) * BWIN + (c >> 2)) * 16 + (r & 3) * 4 + (c & 3)
    rows = place(second, i - CCOLS * second)
    cols = place((i - 48) >> 1, i & 1)
    corner = jnp.where(i < 116, place((i - 112) >> 1, i & 1), -1)
    return jnp.where(i < 48, rows, jnp.where(i < 112, cols, corner))


def picks(source, width):
    lanes = lax.broadcasted_iota(jnp.int32, (source.shape[0], width), 1)
    return (lanes == source).astype(F32).astype(BF16)


def layer_norm(values, scales):
    average = jnp.mean(values, axis=-1, keepdims=True)
    centred = values - average
    spread = jnp.mean(centred * centred, axis=-1, keepdims=True)
    return centred * lax.rsqrt(spread + 1e-05) * scales


def gelu(x):
    return 0.5 * x * (1.0 + jnp.tanh(x * (0.7978845608028654 + 0.035677408136300125 * (x * x))))


def dot(a, b):
    return jnp.dot(a, b, preferred_element_type=F32)


def head_blocks():
    rows = lax.broadcasted_iota(jnp.int32, (QUAD, QUAD), 0) // HEAD_DIM
    lanes = lax.broadcasted_iota(jnp.int32, (QUAD, QUAD), 1) // HEAD_DIM
    return (rows == lanes).astype(F32).astype(BF16)


def segment_max(scores):
    low = lax.broadcasted_iota(jnp.int32, (scores.shape[0], 128), 1) < HEAD_DIM
    out = []
    for t in range(0, QUAD, 128):
        part = scores[:, t : t + 128]
        first = jnp.max(jnp.where(low, part, -3e38), axis=1, keepdims=True)
        second = jnp.max(jnp.where(low, -3e38, part), axis=1, keepdims=True)
        out.append(jnp.where(low, first, second))
    return jnp.concatenate(out, axis=1)


def attend_scores(units, blocks):
    scores = []
    for queries, keys_in, _, bias in units:
        spread = jnp.concatenate([keys_in] * 4, axis=0) * blocks
        score = lax.dot_general(queries, spread, (((1,), (1,)), ((), ())), preferred_element_type=F32) * SCALE
        scores.append(score if bias is None else score + bias)
    return scores


def attend_weights(scores):
    return [jnp.exp2(score - segment_max(score)).astype(BF16) for score in scores]


def attend_values(units, weights, blocks):
    totals = dot(jnp.concatenate(weights, axis=0), blocks)
    mixed = []
    for i, (_, _, values_in, _) in enumerate(units):
        out = dot(weights[i], jnp.concatenate([values_in] * 4, axis=0) * blocks)
        mixed.append((out * (1.0 / totals[i * TOK : i * TOK + TOK])).astype(BF16))
    return mixed


def drive(first, second, order):
    streams = {"F": first, "B": second}
    for name in order:
        next(streams[name])
    for stream in (first, second):
        for _ in stream:
            pass


def section_one(
    x_hbm, wqkv_hbm, wout_hbm, wup_hbm, wdown_hbm, wmerge_hbm,
    rim_rows, rim_cols, rim_corner, flag, gains,
    coarse, send_rows, send_cols, send_corner,
    xs, hcs, wqkv, wout, wup, wdown, wmerge, perm, blocks, qkv, attended, held, merged, sems,
):
    step = pl.program_id(0)
    head = NB * WIN + HALF
    pairs = (
        (x_hbm.at[0:head], xs.at[0:head]), (wqkv_hbm, wqkv), (x_hbm.at[head:ROWS], xs.at[head:ROWS]),
        (wout_hbm, wout), (wup_hbm, wup), (wdown_hbm, wdown), (wmerge_hbm, wmerge),
    )
    copies = [pltpu.make_async_copy(a, b, sems.at[i]) for i, (a, b) in enumerate(pairs)]

    def front(opening):
        if opening:
            copies[0].wait()
        tokens = []
        for i in range(NB):
            top = (step * NB + i) * WIN + HALF
            raw = xs[pl.ds(top, WIN)].reshape(BTOK, C1)
            rim = hcs[pl.ds(pl.multiple_of((step * NB + i) * 32, 32), 32)]
            tokens.append(dot(perm[...], jnp.concatenate([raw, rim], axis=0)))
        tokens = jnp.concatenate(tokens, axis=0)
        yield
        normed = layer_norm(tokens, gains[:, 0:C1]).astype(BF16)
        if opening:
            copies[1].wait()
        yield
        for n in range(0, 3 * C1, 512):
            qkv[:, n : n + 512] = dot(normed, wqkv[:, n : n + 512]).astype(BF16)
            yield
        half_of = lambda axis: (lax.broadcasted_iota(jnp.int32, (TOK, QUAD), axis) >> 3) & 1
        cut = jnp.where((flag[0] == 1) & (step == STEPS - 1), -1e30, 0.0)
        bias = (half_of(0) != half_of(1)).astype(F32) * cut
        for i in range(NB):
            places = [(i * BWIN + w, g * QUAD) for w in range(BWIN) for g in range(C1 // QUAD)]
            units = [
                [qkv[w * TOK : w * TOK + TOK, k * C1 + g : k * C1 + g + QUAD] for k in range(3)]
                + [bias if i == NB - 1 and not opening else None]
                for w, g in places
            ]
            scores = attend_scores(units, blocks[...])
            yield
            weights = attend_weights(scores)
            yield
            for (w, g), mixed in zip(places, attend_values(units, weights, blocks[...])):
                attended[w * TOK : w * TOK + TOK, g : g + QUAD] = mixed
            yield
        if opening:
            copies[3].wait()
        held[...] = (tokens + dot(attended[...], wout[...])).astype(BF16)
        if opening:
            for c in (2, 4, 5):
                copies[c].wait()
        yield

    def back():
        hidden = held[...].astype(F32)
        normed = layer_norm(hidden, gains[:, C1 : 2 * C1]).astype(BF16)
        yield
        total = hidden
        ahead = dot(normed, wup[:, 0:512])
        yield
        for n in range(0, MLP1, 512):
            inner = ahead
            if n + 512 < MLP1:
                ahead = dot(normed, wup[:, n + 512 : n + 1024])
            total = total + dot(gelu(inner).astype(BF16), wdown[n : n + 512, :])
            yield
        refined = total.astype(BF16).astype(F32).reshape(NB * BWIN, 4, 16, C1)
        quads = jnp.concatenate([refined[:, i] for i in range(4)], axis=-1).reshape(NB * BTOK // 4, 4 * C1)
        rows = NB * BTOK // 4
        merged[pl.ds(pl.multiple_of((step - 1) * rows, rows), rows), :] = layer_norm(quads, gains[:, 2 * C1 :]).astype(BF16)
        yield

    @pl.when(step == 0)
    def _():
        for c in copies:
            c.start()
        perm[...] = picks(band_source(), BTOK + 32)
        blocks[...] = head_blocks()
        xs[ROWS : ROWS + HALF] = rim_rows[...]
        hcs[0:240] = rim_cols[16:256]
        hcs[240:256] = rim_corner[...]
        drive(front(True), iter(()), "")

    @pl.when((step > 0) & (step < STEPS))
    def _():
        drive(front(False), back(), ORDER)

    @pl.when(step == STEPS)
    def _():
        drive(iter(()), back(), "")
        copies[6].wait()
        for n in range(0, C2, 256):
            coarse[:, n : n + 256] = dot(merged[...], wmerge[:, n : n + 256]).astype(BF16)
        sent = dot(picks(coarse_send_source(), CTOK), coarse[...]).astype(BF16)
        send_rows[...] = sent[0:48]
        send_cols[...] = sent[48:112]
        send_corner[...] = sent[112:128]


def section_two(
    wqkv_hbm, wout_hbm, own, rim_rows, rim_cols, rim_corner, flag, gain, source, send_source,
    result, send_rows, send_cols, send_corner,
    wqkv, wout, blocks, held, normed, qkv, attended, sems,
):
    groups = C2 // QUAD
    copies = []
    for g in range(groups):
        for k in range(3):
            here = slice(k * C2 + g * QUAD, k * C2 + g * QUAD + QUAD)
            copies.append(pltpu.make_async_copy(wqkv_hbm.at[:, here], wqkv.at[:, here], sems.at[g * 3 + k]))
    copies.append(pltpu.make_async_copy(wout_hbm, wout, sems.at[3 * groups]))
    for c in copies:
        c.start()
    blocks[...] = head_blocks()
    rim = jnp.concatenate([rim_rows[...], rim_cols[...], rim_corner[...]], axis=0)
    for i in range(CBANDS):
        here = slice(i * 192, i * 192 + 192)
        low, high = i * 192, min(i * 192 + 288, CTOK)
        tokens = dot(picks(source[here] - low, high - low), own[low:high]) + dot(picks(source[here] - CTOK, 128), rim)
        held[here] = tokens.astype(BF16)
        normed[here] = layer_norm(tokens, gain[...]).astype(BF16)
    half_of = lambda axis: (lax.broadcasted_iota(jnp.int32, (TOK, QUAD), axis) >> 5) & 1
    bias = (half_of(0) != half_of(1)).astype(F32) * jnp.where(flag[0] == 1, -1e30, 0.0)

    def project(g):
        for k in range(3):
            here = slice(k * C2 + g * QUAD, k * C2 + g * QUAD + QUAD)
            qkv[:, here] = dot(normed[...], wqkv[:, here]).astype(BF16)

    for c in copies[:3]:
        c.wait()
    project(0)
    for c in copies[3:]:
        c.wait()
    for g in range(groups):
        units = [
            [qkv[w * TOK : w * TOK + TOK, k * C2 + g * QUAD : k * C2 + g * QUAD + QUAD] for k in range(3)]
            + [bias if w >= CBWIN * (CBANDS - 1) else None]
            for w in range(CBWIN * CBANDS)
        ]
        scores = attend_scores(units, blocks[...])
        if g + 1 < groups:
            project(g + 1)
        weights = attend_weights(scores)
        for w, mixed in enumerate(attend_values(units, weights, blocks[...])):
            attended[w * TOK : w * TOK + TOK, g * QUAD : g * QUAD + QUAD] = mixed
    for n in range(0, C2, 256):
        here = slice(n, n + 256)
        result[:, here] = (held[:, here].astype(F32) + dot(attended[...], wout[:, here])).astype(BF16)
    sent = dot(picks(send_source[...], CTOK), result[...]).astype(BF16)
    send_rows[...] = sent[0:80]
    send_cols[...] = sent[80:192]
    send_corner[...] = sent[192:208]


def place(result, source, main):
    for i in range(CBANDS):
        here = slice(i * 192, i * 192 + 192)
        low = max(i - 1, 0) * 192
        main[here] = dot(picks(source[here] - low, here.stop - low), result[low : here.stop]).astype(BF16)


def join(main, rows, cols, corner, source, out_hbm, out, sems):
    rim = jnp.concatenate([rows[...], cols[...], corner[...]], axis=0)
    copies = []
    for i in range(CBANDS):
        here = slice(i * 192, i * 192 + 192)
        out[here] = (main[here].astype(F32) + dot(picks(source[here], 208), rim)).astype(BF16)
        copies.append(pltpu.make_async_copy(out.at[here], out_hbm.at[here], sems.at[i]))
        copies[i].start()
    for c in copies:
        c.wait()


HBM = pl.BlockSpec(memory_space=pltpu.HBM)
VM = pl.BlockSpec(memory_space=pltpu.VMEM)
SM = pl.BlockSpec(memory_space=pltpu.SMEM)


def whole(shape):
    return pl.BlockSpec(shape, lambda b: (0,) * len(shape))


def shift(values, axes, back):
    if isinstance(axes, str):
        count = lax.axis_size(axes)
        pairs = [(i, (i + 1) % count) for i in range(count)]
    else:
        lat, lon = (lax.axis_size(a) for a in axes)
        pairs = [(i * lon + j, ((i + 1) % lat) * lon + (j + 1) % lon) for i in range(lat) for j in range(lon)]
    if back:
        pairs = [(b, a) for a, b in pairs]
    return lax.ppermute(values, axes, pairs)


def sds(*shape):
    return jax.ShapeDtypeStruct(shape, BF16)


def run_one(tokens, w_qkv, w_out, w_up, w_down, w_merge, rim_r, rim_c, rim_x, flag, gains):
    return pl.pallas_call(
        section_one,
        grid=(STEPS + 1,),
        out_shape=[sds(CTOK, C2), sds(48, C2), sds(64, C2), sds(16, C2)],
        in_specs=[HBM] * 6 + [VM] * 3
        + [SM, whole((1, 6 * C1))],
        out_specs=[VM] * 4,
        scratch_shapes=[
            pltpu.VMEM((ROWS + HALF, COLS, C1), BF16),
            pltpu.VMEM((256, C1), BF16),
            pltpu.VMEM((C1, 3 * C1), BF16),
            pltpu.VMEM((C1, C1), BF16),
            pltpu.VMEM((C1, MLP1), BF16),
            pltpu.VMEM((MLP1, C1), BF16),
            pltpu.VMEM((4 * C1, C2), BF16),
            pltpu.VMEM((BTOK, BTOK + 32), BF16),
            pltpu.VMEM((QUAD, QUAD), BF16),
            pltpu.VMEM((NB * BTOK, 3 * C1), BF16),
            pltpu.VMEM((NB * BTOK, C1), BF16),
            pltpu.VMEM((NB * BTOK, C1), BF16),
            pltpu.VMEM((CTOK, 4 * C1), BF16),
            pltpu.SemaphoreType.DMA((7,)),
        ],
        compiler_params=pltpu.CompilerParams(vmem_limit_bytes=GRANT << 20),
        name="section_one",
    )(
        tokens, w_qkv, w_out, w_up, w_down, w_merge, rim_r, rim_c, rim_x,
        flag, gains,
    )


def run_two(w_qkv, w_out, coarse, rim_r, rim_c, rim_x, flag, gain):
    return pl.pallas_call(
        section_two,
        grid=(1,),
        out_shape=[sds(CTOK, C2), sds(80, C2), sds(112, C2), sds(16, C2)],
        in_specs=[HBM] * 2 + [VM] * 4 + [SM, whole((1, C2)), whole((CTOK, 1)), whole((208, 1))],
        out_specs=[VM] * 4,
        scratch_shapes=[
            pltpu.VMEM((C2, 3 * C2), BF16),
            pltpu.VMEM((C2, C2), BF16),
            pltpu.VMEM((QUAD, QUAD), BF16),
            pltpu.VMEM((CTOK, C2), BF16),
            pltpu.VMEM((CTOK, C2), BF16),
            pltpu.VMEM((CTOK, 3 * C2), BF16),
            pltpu.VMEM((CTOK, C2), BF16),
            pltpu.SemaphoreType.DMA((13,)),
        ],
        compiler_params=pltpu.CompilerParams(vmem_limit_bytes=48 << 20),
        name="section_two",
    )(
        w_qkv, w_out, coarse, rim_r, rim_c, rim_x, flag, gain.reshape(1, -1),
        jnp.asarray(coarse_source()), jnp.asarray(result_source()[CTOK:]),
    )


def run_place(result):
    return pl.pallas_call(
        place,
        grid=(1,),
        out_shape=sds(CTOK, C2),
        in_specs=[VM, whole((CTOK, 1))],
        out_specs=VM,
        cost_estimate=pl.CostEstimate(flops=2 * CTOK * 384 * C2, bytes_accessed=5 << 20, transcendentals=0),
        compiler_params=pltpu.CompilerParams(vmem_limit_bytes=32 << 20),
        name="place",
    )(result, jnp.asarray(result_source()[:CTOK]))


def run_join(main, rim_r, rim_c, rim_x):
    return pl.pallas_call(
        join,
        grid=(1,),
        out_shape=sds(CTOK, C2),
        in_specs=[VM, VM, VM, VM, whole((CTOK, 1))],
        out_specs=HBM,
        scratch_shapes=[pltpu.VMEM((CTOK, C2), BF16), pltpu.SemaphoreType.DMA((CBANDS,))],
        compiler_params=pltpu.CompilerParams(vmem_limit_bytes=32 << 20),
        name="join",
    )(main, rim_r, rim_c, rim_x, jnp.asarray(rim_source()))


def on_device(
    tokens, gain_attn1, w_qkv1, w_out1, gain_mlp1, w_up, w_down, gain_merge, w_merge, gain_attn2, w_qkv2, w_out2,
):
    flag = (lax.axis_index("lat") == lax.axis_size("lat") - 1).astype(jnp.int32).reshape(1)
    strip = lax.optimization_barrier(tokens[:, 0:HALF].reshape(256, C1))
    rim_c = shift(strip, "lon", True)
    rim_r = shift(tokens[0:HALF], "lat", True)
    rim_x = shift(strip[0:16], ("lat", "lon"), True)
    coarse, s_r, s_c, s_x = run_one(
        tokens, w_qkv1, w_out1, w_up, w_down, w_merge, rim_r, rim_c, rim_x, flag,
        jnp.concatenate([gain_attn1, gain_mlp1, gain_merge]).reshape(1, -1),
    )
    r_r = shift(s_r, "lat", True)
    r_c = shift(s_c, "lon", True)
    r_x = shift(s_x, ("lat", "lon"), True)
    result, s_r, s_c, s_x = run_two(w_qkv2, w_out2, coarse, r_r, r_c, r_x, flag, gain_attn2)
    r_r = shift(s_r, "lat", False)
    r_c = shift(s_c, "lon", False)
    r_x = shift(s_x, ("lat", "lon"), False)
    return run_join(run_place(result), r_r, r_c, r_x).reshape(CROWS, CCOLS, C2)


def solution(mesh):
    in_specs = (P("lat", "lon", None),) + (P(),) * 11
    return jax.shard_map(
        on_device, mesh=mesh, in_specs=in_specs, out_specs=P("lat", "lon", None), check_vma=False
    )
```
